512 devices in a mesh: row: 32 (over y, x, core), col: 16 (over z).
Axes of the slice: x: 4, y: 4, z: 16, core: 2. Of those that a mesh axis runs over, the one named last changes fastest.
Arguments:
- columns_x: bfloat16 [32, 262144], P(None, ('row', 'col')), may hold values from -6 to 6
- col_basis: bfloat16 [1024, 64, 256], P(('row', 'col')), may hold values from -0.375 to 0.375
- col_links: bfloat16 [1024, 4096], P(('row', 'col')), may hold values from -0.5 to 0.5
- col_top_links: bfloat16 [16, 48, 4096], P('col'), may hold values from -0.5 to 0.5
- row_basis: bfloat16 [1024, 64, 256], P(('row', 'col')), may hold values from -0.75 to 0.75
- row_links: bfloat16 [32, 56, 4096], P('row'), may hold values from -0.5 to 0.5
- coupling: bfloat16 [65536, 4096], P(('row', 'col')), may hold values from -0.09375 to 0.09375
- coupling_rows: int32 [2048, 32], P(('row', 'col')), may hold values from 0 to 31, as said below
- coupling_cols: int32 [2048, 32], P(('row', 'col')), may hold values from 0 to 63, as said below
- near_blocks: bfloat16 [4096, 256, 256], P(('row', 'col')), may hold values from -0.1875 to 0.1875
- near_rows: int32 [4096], P(('row', 'col')), may hold values from 0 to 1
- near_cols: int32 [4096], P(('row', 'col')), may hold values from 0 to 1
Outputs:
- products: bfloat16 [32, 262144], P(None, ('row', 'col'))
The draws below stay inside these ranges and needn't reach their ends.
Inputs may be any that keep to these rules, and one draw needn't show every extreme that they name: `coupling_rows`: in list row j the level is l = j mod 4, and the entry names a row cluster of level l of the row tree of the device's row index, below 32 / 2**l. `coupling_cols`: in list row j the level is l = j mod 4, and the entry names a column cluster of level l of the column tree of the device's col index, below 64 / 2**l. `near_rows`: a row leaf of the device's own part, numbered within it. `near_cols`: a column leaf of the device's own part, numbered within it.
All inputs are finite; a program needn't handle non-finite values.
Results may differ from the reference program's by a relative error of at most 0.02.
Values may be sent and summed in bfloat16 or wider, within the bound.
No kernel may reach another device: no remote copies, remote signals or barrier semaphores. Data moves between devices by JAX's collectives and lax.ppermute only.
A program may use at most 64 MiB of HBM per device.

```python
import jax
import jax.numpy as jnp
from jax import lax

NV = 32
K = 64
LEAF = 256
LV = 2
BPL = 32
NEAR = 8
LD = 2
NL = 4
RCL = 32
CCL = 64
ROWLINKS = 56
TOPCOL = 48
LISTS = 2048
NROWS = 262144
NCOLS = 262144
N_ROW = 32
N_COL = 16


def level_indices(key, leaves):
    raw = jax.random.randint(key, (LISTS, BPL), 0, 1 << 30)
    depth = (jnp.arange(LISTS, dtype=jnp.int32) % NL)[:, None]
    count = jnp.right_shift(jnp.full((LISTS, 1), leaves, jnp.int32), depth)
    picked = raw % count
    marked = jax.random.randint(jax.random.fold_in(key, 7), (LISTS, 1), 0, BPL)
    slots = jnp.arange(BPL, dtype=jnp.int32)[None, :]
    return jnp.where(slots == marked, count - 1, picked).astype(jnp.int32)


def draw_coupling_rows(key, part):
    key = jax.random.fold_in(key, 11)
    return level_indices(key, RCL)


def draw_coupling_cols(key, part):
    key = jax.random.fold_in(key, 23)
    return level_indices(key, CCL)


def set_ends(values, stream_key, low, high):
    place = [jax.random.randint(jax.random.fold_in(stream_key, axis), (), 0, length) for axis, length in enumerate(values.shape)]
    main_axis = values.shape.index(max(values.shape))
    neighbour = place[:main_axis] + [(place[main_axis] + 1) % values.shape[main_axis]] + place[main_axis + 1:]
    return values.at[tuple(place)].set(low).at[tuple(neighbour)].set(high)


def shard_levels(key, extent, split, low, high):
    loudness, own = 1.0, jax.random.fold_in(key, 6)
    for position, blocks in split:
        steps = jnp.exp(jax.random.uniform(jax.random.fold_in(own, position), (blocks,), jnp.float32, low / len(split), high / len(split)))
        loudness = loudness * jnp.repeat(steps, extent[position] // blocks).reshape([-1 if axis == position else 1 for axis in range(len(extent))])
    return loudness


def scatter_about(own_key, shape, spread, most, split=(), held_as=jnp.bfloat16):
    values = jax.random.normal(own_key, shape, jnp.float32) * spread
    if len(split) > 0:
        values = shard_levels(own_key, shape, split, -0.22, 0.18) * values
    return jnp.clip(values, min=-most, max=most).astype(held_as)


def setup_inputs(seed: int = 0) -> dict:
    key_list = jax.random.split(jax.random.key(seed), 13)
    return {
        "columns_x": scatter_about(key_list[0], (NV, NCOLS), 1.0, 6.0, ((1, 512),)),
        "col_basis": scatter_about(key_list[1], (NCOLS // LEAF, K, LEAF), LEAF ** -0.5, 0.375, ((0, 512),)),
        "col_links": scatter_about(key_list[2], (N_ROW * N_COL * (2 * LD - 2), K * K), (2 * K) ** -0.5, 0.5, ((0, 512),)),
        "col_top_links": scatter_about(key_list[3], (N_COL, TOPCOL, K * K), (2 * K) ** -0.5, 0.5, ((0, 16),)),
        "row_basis": scatter_about(key_list[4], (NROWS // LEAF, K, LEAF), K ** -0.5, 0.75, ((0, 512),)),
        "row_links": scatter_about(key_list[5], (N_ROW, ROWLINKS, K * K), (2 * K) ** -0.5, 0.5, ((0, 32),)),
        "coupling": scatter_about(key_list[6], (LISTS * BPL, K * K), (K * NL * BPL // LD) ** -0.5, 0.09375, ((0, 512),)),
        "coupling_rows": draw_coupling_rows(jax.random.fold_in(key_list[12], 71), 0),
        "coupling_cols": draw_coupling_cols(jax.random.fold_in(key_list[12], 71), 0),
        "near_blocks": scatter_about(key_list[9], (N_ROW * N_COL * NEAR, LEAF, LEAF), (LEAF * NEAR // LD) ** -0.5, 0.1875, ((0, 512),)),
        "near_rows": set_ends(jax.random.randint(key_list[10], (N_ROW * N_COL * NEAR,), 0, LD), jax.random.fold_in(key_list[10], 1), 0, LD - 1).astype(jnp.int32),
        "near_cols": set_ends(jax.random.randint(key_list[11], (N_ROW * N_COL * NEAR,), 0, LD), jax.random.fold_in(key_list[11], 1), 0, LD - 1).astype(jnp.int32),
    }


def pair_sum(children, links):
    terms = jnp.einsum('...pnk,...pkj->...pnj', children.astype(jnp.float32), links.astype(jnp.float32))
    shape = terms.shape
    return terms.reshape(shape[:-3] + (shape[-3] // 2, 2) + shape[-2:]).sum(axis=-3)


def pick_rows(source, index):
    return source[index]


def reference(columns_x, col_basis, col_links, col_top_links, row_basis, row_links, coupling, coupling_rows, coupling_cols, near_blocks, near_rows, near_cols):
    sites_x = columns_x.reshape(NV, N_ROW, N_COL, LD, LEAF).transpose(1, 2, 3, 0, 4)
    bases = col_basis.reshape(N_ROW, N_COL, LD, K, LEAF)
    moments = jnp.einsum('rcinl,rcikl->rcink', sites_x.astype(jnp.float32), bases.astype(jnp.float32)).astype(jnp.bfloat16)
    links = col_links.reshape(N_ROW, N_COL, 2 * LD - 2, K, K)
    trees = [moments.transpose(1, 0, 2, 3, 4).reshape(N_COL, CCL, NV, K)]
    offset = 0
    for depth in range(1, LV):
        count = LD >> (depth - 1)
        moments = pair_sum(moments, links[:, :, offset:offset + count]).astype(jnp.bfloat16)
        offset += count
        trees.append(moments.transpose(1, 0, 2, 3, 4).reshape(N_COL, CCL >> depth, NV, K))
    top_links = col_top_links.reshape(N_COL, TOPCOL, K, K)
    current = trees[-1]
    offset = 0
    for depth in range(LV, NL):
        count = current.shape[1]
        current = pair_sum(current, top_links[:, offset:offset + count]).astype(jnp.bfloat16)
        offset += count
        trees.append(current)

    def one_tree(pieces):
        tree_blocks, tree_rows, tree_cols, tree_links, tree_bases, tree_sites, tree_near, near_targets, near_sources = pieces
        totals = []
        for depth in range(NL):
            picked = jax.vmap(pick_rows)(trees[depth], tree_cols[:, depth])
            terms = jnp.einsum('cbnk,cbkj->cbnj', picked.astype(jnp.float32), tree_blocks[:, depth].astype(jnp.float32))
            totals.append(jax.ops.segment_sum(terms.reshape(N_COL * BPL, NV, K), tree_rows[:, depth].reshape(N_COL * BPL), num_segments=RCL >> depth))
        running = totals[NL - 1]
        for depth in range(NL - 2, -1, -1):
            count = RCL >> depth
            start = 2 * (RCL - count)
            parents = jnp.repeat(running, 2, axis=0)
            running = totals[depth] + jnp.einsum('pnk,pkj->pnj', parents, tree_links[start:start + count].astype(jnp.float32), precision=lax.Precision.HIGHEST)
        leaf_local = running.astype(jnp.bfloat16).reshape(N_COL, LD, NV, K)
        distant = jnp.einsum('cink,cikl->cinl', leaf_local.astype(jnp.float32), tree_bases.astype(jnp.float32))
        chosen = jax.vmap(pick_rows)(tree_sites, near_sources)
        nearby = jnp.einsum('cbnl,cblm->cbnm', chosen.astype(jnp.float32), tree_near.astype(jnp.float32))
        summed = jax.vmap(lambda values, index: jax.ops.segment_sum(values, index, num_segments=LD))(nearby, near_targets)
        return (distant + summed).astype(jnp.bfloat16)

    pieces = (coupling.reshape(N_ROW, N_COL, NL, BPL, K, K),
              coupling_rows.reshape(N_ROW, N_COL, NL, BPL),
              coupling_cols.reshape(N_ROW, N_COL, NL, BPL),
              row_links.reshape(N_ROW, ROWLINKS, K, K),
              row_basis.reshape(N_ROW, N_COL, LD, K, LEAF),
              sites_x,
              near_blocks.reshape(N_ROW, N_COL, NEAR, LEAF, LEAF),
              near_rows.reshape(N_ROW, N_COL, NEAR),
              near_cols.reshape(N_ROW, N_COL, NEAR))
    result = lax.map(one_tree, pieces)
    return result.transpose(3, 0, 1, 2, 4).reshape(NV, NROWS)
```

```python
import jax
import jax.numpy as jnp
from jax import lax
from jax.experimental import pallas as pl
from jax.experimental.pallas import tpu as pltpu
from jax.sharding import PartitionSpec as P

F32 = jnp.float32
BF16 = jnp.bfloat16


def dot(a, b):
    return jnp.dot(a, b, preferred_element_type=F32)


def vmem():
    return pl.BlockSpec(memory_space=pltpu.VMEM)


def smem():
    return pl.BlockSpec(memory_space=pltpu.SMEM)


def moments_kernel(x_ref, basis_ref, links_ref, out_ref):
    leaves = []
    for i in range(2):
        moment = lax.dot_general(
            x_ref[:, 256 * i : 256 * (i + 1)],
            basis_ref[i],
            (((1,), (1,)), ((), ())),
            preferred_element_type=F32,
        )
        leaves.append(moment.astype(BF16))
    parent = dot(leaves[0], links_ref[0]) + dot(leaves[1], links_ref[1])
    low = jnp.concatenate(leaves, axis=1)
    high = jnp.concatenate([parent[:16], parent[16:]], axis=1).astype(BF16)
    for r in range(out_ref.shape[0]):
        out_ref[r, 0:32, :] = low
        out_ref[r, 32:48, :] = high


def tree_kernel(rows_ref, cols_ref, got_ref, top_ref, coupling_ref, links_ref, out_ref, mom, acc):
    for a in range(32):
        both = got_ref[a, 0:32, :]
        mom[2 * a] = both[:, 0:64]
        mom[2 * a + 1] = both[:, 64:128]
        parent = got_ref[a, 32:48, :]
        mom[64 + a, 0:16] = parent[:, 0:64]
        mom[64 + a, 16:32] = parent[:, 64:128]
    for p in range(16):
        total = dot(mom[64 + 2 * p], top_ref[2 * p]) + dot(mom[65 + 2 * p], top_ref[2 * p + 1])
        mom[96 + p] = total.astype(BF16)
    for p in range(8):
        total = dot(mom[96 + 2 * p], top_ref[32 + 2 * p]) + dot(mom[97 + 2 * p], top_ref[33 + 2 * p])
        mom[112 + p] = total.astype(BF16)
    acc[...] = jnp.zeros_like(acc)
    for depth in range(4):
        first_col = 128 - (128 >> depth)
        first_row = 64 - (64 >> depth)
        for s in range(32):
            q = first_col + cols_ref[depth, s]
            p = first_row + rows_ref[depth, s]
            acc[p] += dot(mom[q], coupling_ref[depth * 32 + s])
    for depth in (2, 1, 0):
        count = 32 >> depth
        first = 64 - (64 >> depth)
        start = 2 * (32 - count)
        for p in range(count):
            parent = acc[first + count + p // 2].astype(BF16)
            acc[first + p] += dot(parent, links_ref[start + p])
    for b in range(16):
        out_ref[b, :, 0:64] = acc[2 * b].astype(BF16)
        out_ref[b, :, 64:128] = acc[2 * b + 1].astype(BF16)


def output_kernel(rows_ref, cols_ref, got_ref, basis_ref, x_ref, near_ref, out_ref, acc):
    total = got_ref[0].astype(F32)
    for b in range(1, got_ref.shape[0]):
        total += got_ref[b].astype(F32)
    leaf_local = total.astype(BF16)
    for i in range(2):
        acc[i] = dot(leaf_local[:, 64 * i : 64 * (i + 1)], basis_ref[i])
    for s in range(8):
        start = pl.multiple_of(cols_ref[s] * 256, 256)
        acc[rows_ref[s]] += dot(x_ref[:, pl.ds(start, 256)], near_ref[s])
    for i in range(2):
        out_ref[:, 256 * i : 256 * (i + 1)] = acc[i].astype(BF16)


def local(
    columns_x,
    col_basis,
    col_links,
    col_top_links,
    row_basis,
    row_links,
    coupling,
    coupling_rows,
    coupling_cols,
    near_blocks,
    near_rows,
    near_cols,
):
    message = pl.pallas_call(
        moments_kernel,
        out_shape=jax.ShapeDtypeStruct((32, 48, 128), BF16),
        in_specs=[vmem()] * 3,
        out_specs=vmem(),
        name="moments",
    )(columns_x, col_basis, col_links.reshape(2, 64, 64))
    gathered = lax.all_to_all(message, "row", 0, 0)
    partials = pl.pallas_call(
        tree_kernel,
        out_shape=jax.ShapeDtypeStruct((16, 32, 128), BF16),
        in_specs=[smem()] * 2 + [vmem()] * 4,
        out_specs=vmem(),
        scratch_shapes=[pltpu.VMEM((120, 32, 64), BF16), pltpu.VMEM((60, 32, 64), F32)],
        compiler_params=pltpu.CompilerParams(vmem_limit_bytes=32 * 1024 * 1024),
        name="trees",
    )(
        coupling_rows,
        coupling_cols,
        gathered,
        col_top_links[0].reshape(48, 64, 64),
        coupling.reshape(128, 64, 64),
        row_links[0].reshape(56, 64, 64),
    )
    scattered = lax.all_to_all(partials, "col", 0, 0)
    return pl.pallas_call(
        output_kernel,
        out_shape=jax.ShapeDtypeStruct((32, 512), BF16),
        in_specs=[smem()] * 2 + [vmem()] * 4,
        out_specs=vmem(),
        scratch_shapes=[pltpu.VMEM((2, 32, 256), F32)],
        compiler_params=pltpu.CompilerParams(vmem_limit_bytes=16 * 1024 * 1024),
        name="outputs",
    )(near_rows, near_cols, scattered, row_basis, columns_x, near_blocks)


def solution(mesh):
    in_specs = (
        P(None, ("row", "col")),
        P(("row", "col"), None, None),
        P(("row", "col"), None),
        P("col", None, None),
        P(("row", "col"), None, None),
        P("row", None, None),
        P(("row", "col"), None),
        P(("row", "col"), None),
        P(("row", "col"), None),
        P(("row", "col"), None, None),
        P(("row", "col")),
        P(("row", "col")),
    )
    out_specs = P(None, ("row", "col"))
    return jax.shard_map(local, mesh=mesh, in_specs=in_specs, out_specs=out_specs, check_vma=False)
```

```python
import jax
import jax.numpy as jnp
from jax import lax
from jax.experimental import pallas as pl
from jax.experimental.pallas import tpu as pltpu
from jax.sharding import PartitionSpec as P

F32 = jnp.float32
BF16 = jnp.bfloat16


def dot(a, b):
    return jnp.dot(a, b, preferred_element_type=F32)


def vmem():
    return pl.BlockSpec(memory_space=pltpu.VMEM)


def smem():
    return pl.BlockSpec(memory_space=pltpu.SMEM)


def out_vmem(shape, dtype):
    return pltpu.VMEM(shape, dtype)


def moments_kernel(x_ref, basis_ref, links_ref, out_ref):
    links = links_ref[...].reshape(2, 64, 64)
    leaves = []
    for i in range(2):
        moment = lax.dot_general(
            x_ref[:, 256 * i : 256 * (i + 1)],
            basis_ref[i],
            (((1,), (1,)), ((), ())),
            preferred_element_type=F32,
        )
        leaves.append(moment.astype(BF16))
    parent = dot(leaves[0], links[0]) + dot(leaves[1], links[1])
    low = jnp.concatenate(leaves, axis=1)
    high = jnp.concatenate([parent[:16], parent[16:]], axis=1).astype(BF16)
    for r in range(out_ref.shape[0]):
        out_ref[r, 0:32, :] = low
        out_ref[r, 32:48, :] = high


def beside(matrices):
    half = matrices.shape[0] // 2
    return jnp.concatenate([matrices[:half], matrices[half:]], axis=2)


def matrix(ref, j):
    side, place = divmod(j, ref.shape[0])
    return ref[place, :, 64 * side : 64 * (side + 1)]


def unpack_kernel(coupling_ref, top_ref, links_ref, rows_ref, cols_ref, blocks_ref, up_ref, down_ref, lists_ref):
    lists_ref[0:4, 0:32] = rows_ref[...]
    lists_ref[4:8, 0:32] = cols_ref[...]
    blocks_ref[...] = beside(coupling_ref[...].reshape(128, 64, 64))
    up_ref[...] = beside(top_ref[0].reshape(48, 64, 64))
    down_ref[...] = beside(links_ref[0].reshape(56, 64, 64))


def tree_kernel(
    lists_in, got_ref, top_ref, coupling_ref, links_ref, out_ref,
    mom0, mom1, mom2, mom3, acc0, acc1, acc2, acc3, lists_ref, sem,
):
    mom, acc = (mom0, mom1, mom2, mom3), (acc0, acc1, acc2, acc3)
    copy = pltpu.make_async_copy(lists_in, lists_ref, sem)
    copy.start()
    for a in range(32):
        both = got_ref[a, 0:32, :]
        mom0[2 * a] = both[:, 0:64]
        mom0[2 * a + 1] = both[:, 64:128]
        parent = got_ref[a, 32:48, :]
        mom1[a, 0:16] = parent[:, 0:64]
        mom1[a, 16:32] = parent[:, 64:128]
    for depth in range(4):
        acc[depth][...] = jnp.zeros_like(acc[depth])
    for p in range(16):
        mom2[p] = (dot(mom1[2 * p], matrix(top_ref, 2 * p)) + dot(mom1[2 * p + 1], matrix(top_ref, 2 * p + 1))).astype(BF16)
    for p in range(8):
        mom3[p] = (dot(mom2[2 * p], matrix(top_ref, 32 + 2 * p)) + dot(mom2[2 * p + 1], matrix(top_ref, 33 + 2 * p))).astype(BF16)
    copy.wait()
    for s in range(32):
        for depth in range(4):
            q, p = lists_ref[4 + depth, s], lists_ref[depth, s]
            acc[depth][p] += dot(mom[depth][q], matrix(coupling_ref, depth * 32 + s))
    for depth in (2, 1, 0):
        count = 32 >> depth
        start = 2 * (32 - count)
        for p in range(count):
            acc[depth][p] += dot(acc[depth + 1][p // 2].astype(BF16), matrix(links_ref, start + p))
    for b in range(16):
        out_ref[b, :, 0:64] = acc0[2 * b].astype(BF16)
        out_ref[b, :, 64:128] = acc0[2 * b + 1].astype(BF16)


def near_kernel(rows_ref, cols_ref, x_ref, near_ref, out_ref):
    out_ref[...] = jnp.zeros_like(out_ref)
    for s in range(8):
        start = pl.multiple_of(cols_ref[s] * 256, 256)
        out_ref[rows_ref[s]] += dot(x_ref[:, pl.ds(start, 256)], near_ref[s])


def output_kernel(got_ref, basis_ref, near_ref, out_ref):
    total = got_ref[0].astype(F32)
    for b in range(1, got_ref.shape[0]):
        total += got_ref[b].astype(F32)
    leaf_local = total.astype(BF16)
    for i in range(2):
        distant = dot(leaf_local[:, 64 * i : 64 * (i + 1)], basis_ref[i])
        out_ref[:, 256 * i : 256 * (i + 1)] = (distant + near_ref[i]).astype(BF16)


def local(
    columns_x,
    col_basis,
    col_links,
    col_top_links,
    row_basis,
    row_links,
    coupling,
    coupling_rows,
    coupling_cols,
    near_blocks,
    near_rows,
    near_cols,
):
    message = pl.pallas_call(
        moments_kernel,
        out_shape=jax.ShapeDtypeStruct((32, 48, 128), BF16),
        in_specs=[vmem()] * 3,
        out_specs=vmem(),
        name="moments",
    )(columns_x, col_basis, col_links)
    gathered = lax.all_to_all(message, "row", 0, 0)
    blocks, up, down, lists = pl.pallas_call(
        unpack_kernel,
        out_shape=[out_vmem((count, 64, 128), BF16) for count in (64, 24, 28)] + [out_vmem((8, 128), jnp.int32)],
        in_specs=[vmem()] * 5,
        out_specs=[vmem()] * 4,
        compiler_params=pltpu.CompilerParams(vmem_limit_bytes=16 * 1024 * 1024),
        cost_estimate=pl.CostEstimate(flops=0, bytes_accessed=8_000_000, transcendentals=0),
        name="unpack",
    )(coupling, col_top_links, row_links, coupling_rows, coupling_cols)
    nearby = pl.pallas_call(
        near_kernel,
        out_shape=out_vmem((2, 32, 256), F32),
        in_specs=[smem()] * 2 + [vmem()] * 2,
        out_specs=vmem(),
        compiler_params=pltpu.CompilerParams(vmem_limit_bytes=16 * 1024 * 1024),
        cost_estimate=pl.CostEstimate(flops=33_554_432, bytes_accessed=1_200_000, transcendentals=0),
        name="near",
    )(near_rows, near_cols, columns_x, near_blocks)
    partials = pl.pallas_call(
        tree_kernel,
        out_shape=jax.ShapeDtypeStruct((16, 32, 128), BF16),
        in_specs=[vmem()] * 5,
        out_specs=vmem(),
        scratch_shapes=[pltpu.VMEM((64 >> depth, 32, 64), BF16) for depth in range(4)]
        + [pltpu.VMEM((32 >> depth, 32, 64), F32) for depth in range(4)]
        + [pltpu.SMEM((8, 128), jnp.int32), pltpu.SemaphoreType.DMA],
        compiler_params=pltpu.CompilerParams(vmem_limit_bytes=16 * 1024 * 1024),
        name="trees",
    )(lists, gathered, up, blocks, down)
    scattered = lax.all_to_all(partials, "col", 0, 0)
    return pl.pallas_call(
        output_kernel,
        out_shape=jax.ShapeDtypeStruct((32, 512), BF16),
        in_specs=[vmem()] * 3,
        out_specs=vmem(),
        compiler_params=pltpu.CompilerParams(vmem_limit_bytes=8 * 1024 * 1024),
        name="outputs",
    )(scattered, row_basis, nearby)


def solution(mesh):
    in_specs = (
        P(None, ("row", "col")),
        P(("row", "col"), None, None),
        P(("row", "col"), None),
        P("col", None, None),
        P(("row", "col"), None, None),
        P("row", None, None),
        P(("row", "col"), None),
        P(("row", "col"), None),
        P(("row", "col"), None),
        P(("row", "col"), None, None),
        P(("row", "col")),
        P(("row", "col")),
    )
    out_specs = P(None, ("row", "col"))
    return jax.shard_map(local, mesh=mesh, in_specs=in_specs, out_specs=out_specs, check_vma=False)
```

```python
import jax
import jax.numpy as jnp
from jax import lax
from jax.experimental import pallas as pl
from jax.experimental.pallas import tpu as pltpu
from jax.sharding import PartitionSpec as P

F32 = jnp.float32
BF16 = jnp.bfloat16


def dot(a, b):
    return jnp.dot(a, b, preferred_element_type=F32)


def vmem():
    return pl.BlockSpec(memory_space=pltpu.VMEM)


def smem():
    return pl.BlockSpec(memory_space=pltpu.SMEM)


def out_vmem(shape, dtype):
    return pltpu.VMEM(shape, dtype)


def moments_kernel(x_ref, basis_ref, links_ref, out_ref):
    links = links_ref[...].reshape(2, 64, 64)
    leaves = []
    for i in range(2):
        moment = lax.dot_general(
            x_ref[:, 256 * i : 256 * (i + 1)],
            basis_ref[i],
            (((1,), (1,)), ((), ())),
            preferred_element_type=F32,
        )
        leaves.append(moment.astype(BF16))
    parent = dot(leaves[0], links[0]) + dot(leaves[1], links[1])
    low = jnp.concatenate(leaves, axis=1)
    high = jnp.concatenate([parent[:16], parent[16:]], axis=1).astype(BF16)
    for r in range(out_ref.shape[0]):
        out_ref[r, 0:32, :] = low
        out_ref[r, 32:48, :] = high


def beside(matrices):
    half = matrices.shape[0] // 2
    return jnp.concatenate([matrices[:half], matrices[half:]], axis=2)


def matrix(ref, j):
    side, place = divmod(j, ref.shape[0])
    return ref[place, :, 64 * side : 64 * (side + 1)]


def unpack_kernel(coupling_ref, top_ref, links_ref, rows_ref, cols_ref, blocks_ref, up_ref, down_ref, lists_ref):
    lists_ref[0:4, 0:32] = rows_ref[...]
    lists_ref[4:8, 0:32] = cols_ref[...]
    blocks_ref[...] = beside(coupling_ref[...].reshape(128, 64, 64))
    up_ref[...] = beside(top_ref[0].reshape(48, 64, 64))
    links = links_ref[0].reshape(56, 64, 64)
    for b in range(16):
        one = jnp.concatenate([links[2 * b], links[2 * b + 1]], axis=1)
        two = dot(links[32 + b], one).astype(BF16)
        three = dot(links[48 + b // 2], two).astype(BF16)
        down_ref[b, 0:64, :] = one
        down_ref[b, 64:128, :] = two
        down_ref[b, 128:192, :] = three


def tree_kernel(
    lists_in, got_ref, top_ref, coupling_ref, down_ref, out_ref,
    mom0, mom1, mom2, mom3, acc0, acc1, acc2, acc3, lists_ref, sem,
):
    mom, acc = (mom0, mom1, mom2, mom3), (acc0, acc1, acc2, acc3)
    copy = pltpu.make_async_copy(lists_in, lists_ref, sem)
    copy.start()
    for a in range(32):
        parent = got_ref[a, 32:48, :]
        mom1[a, 0:16] = parent[:, 0:64]
        mom1[a, 16:32] = parent[:, 64:128]
    for p in range(16):
        mom2[p] = (dot(mom1[2 * p], matrix(top_ref, 2 * p)) + dot(mom1[2 * p + 1], matrix(top_ref, 2 * p + 1))).astype(BF16)
    for a in range(32):
        both = got_ref[a, 0:32, :]
        mom0[2 * a] = both[:, 0:64]
        mom0[2 * a + 1] = both[:, 64:128]
    for p in range(8):
        mom3[p] = (dot(mom2[2 * p], matrix(top_ref, 32 + 2 * p)) + dot(mom2[2 * p + 1], matrix(top_ref, 33 + 2 * p))).astype(BF16)
    for depth in range(4):
        acc[depth][...] = jnp.zeros_like(acc[depth])
    copy.wait()
    for s in range(32):
        for depth in range(4):
            q, p = lists_ref[4 + depth, s], lists_ref[depth, s]
            acc[depth][p] += dot(mom[depth][q], matrix(coupling_ref, depth * 32 + s))
    for b in range(16):
        upper = jnp.concatenate([acc1[b], acc2[b // 2], acc3[b // 4]], axis=1).astype(BF16)
        own = jnp.concatenate([acc0[2 * b], acc0[2 * b + 1]], axis=1)
        out_ref[b] = (own + dot(upper, down_ref[b])).astype(BF16)


def near_kernel(rows_ref, cols_ref, x_ref, near_ref, out_ref):
    out_ref[...] = jnp.zeros_like(out_ref)
    for s in range(8):
        start = pl.multiple_of(cols_ref[s] * 256, 256)
        out_ref[rows_ref[s]] += dot(x_ref[:, pl.ds(start, 256)], near_ref[s])


def output_kernel(got_ref, basis_ref, near_ref, out_ref):
    total = got_ref[0].astype(F32)
    for b in range(1, got_ref.shape[0]):
        total += got_ref[b].astype(F32)
    leaf_local = total.astype(BF16)
    for i in range(2):
        distant = dot(leaf_local[:, 64 * i : 64 * (i + 1)], basis_ref[i])
        out_ref[:, 256 * i : 256 * (i + 1)] = (distant + near_ref[i]).astype(BF16)


def local(
    columns_x,
    col_basis,
    col_links,
    col_top_links,
    row_basis,
    row_links,
    coupling,
    coupling_rows,
    coupling_cols,
    near_blocks,
    near_rows,
    near_cols,
):
    message = pl.pallas_call(
        moments_kernel,
        out_shape=jax.ShapeDtypeStruct((32, 48, 128), BF16),
        in_specs=[vmem()] * 3,
        out_specs=vmem(),
        name="moments",
    )(columns_x, col_basis, col_links)
    gathered = lax.all_to_all(message, "row", 0, 0)
    blocks, up, down, lists = pl.pallas_call(
        unpack_kernel,
        out_shape=[
            out_vmem((64, 64, 128), BF16),
            out_vmem((24, 64, 128), BF16),
            out_vmem((16, 192, 128), BF16),
            out_vmem((8, 128), jnp.int32),
        ],
        in_specs=[vmem()] * 5,
        out_specs=[vmem()] * 4,
        compiler_params=pltpu.CompilerParams(vmem_limit_bytes=16 * 1024 * 1024),
        cost_estimate=pl.CostEstimate(flops=0, bytes_accessed=8_000_000, transcendentals=0),
        name="unpack",
    )(coupling, col_top_links, row_links, coupling_rows, coupling_cols)
    nearby = pl.pallas_call(
        near_kernel,
        out_shape=out_vmem((2, 32, 256), F32),
        in_specs=[smem()] * 2 + [vmem()] * 2,
        out_specs=vmem(),
        compiler_params=pltpu.CompilerParams(vmem_limit_bytes=16 * 1024 * 1024),
        cost_estimate=pl.CostEstimate(flops=33_554_432, bytes_accessed=1_200_000, transcendentals=0),
        name="near",
    )(near_rows, near_cols, columns_x, near_blocks)
    gathered, nearby = lax.optimization_barrier((gathered, nearby))
    partials = pl.pallas_call(
        tree_kernel,
        out_shape=jax.ShapeDtypeStruct((16, 32, 128), BF16),
        in_specs=[vmem()] * 5,
        out_specs=vmem(),
        scratch_shapes=[pltpu.VMEM((64 >> depth, 32, 64), BF16) for depth in range(4)]
        + [pltpu.VMEM((32 >> depth, 32, 64), F32) for depth in range(4)]
        + [pltpu.SMEM((8, 128), jnp.int32), pltpu.SemaphoreType.DMA],
        compiler_params=pltpu.CompilerParams(vmem_limit_bytes=16 * 1024 * 1024),
        name="trees",
    )(lists, gathered, up, blocks, down)
    scattered = lax.all_to_all(partials, "col", 0, 0)
    return pl.pallas_call(
        output_kernel,
        out_shape=jax.ShapeDtypeStruct((32, 512), BF16),
        in_specs=[vmem()] * 3,
        out_specs=vmem(),
        compiler_params=pltpu.CompilerParams(vmem_limit_bytes=8 * 1024 * 1024),
        name="outputs",
    )(scattered, row_basis, nearby)


def solution(mesh):
    in_specs = (
        P(None, ("row", "col")),
        P(("row", "col"), None, None),
        P(("row", "col"), None),
        P("col", None, None),
        P(("row", "col"), None, None),
        P("row", None, None),
        P(("row", "col"), None),
        P(("row", "col"), None),
        P(("row", "col"), None),
        P(("row", "col"), None, None),
        P(("row", "col")),
        P(("row", "col")),
    )
    out_specs = P(None, ("row", "col"))
    return jax.shard_map(local, mesh=mesh, in_specs=in_specs, out_specs=out_specs, check_vma=False)
```

```python
import jax
import jax.numpy as jnp
from jax import lax
from jax.experimental import pallas as pl
from jax.experimental.pallas import tpu as pltpu
from jax.sharding import PartitionSpec as P

F32 = jnp.float32
BF16 = jnp.bfloat16


def dot(a, b):
    return jnp.dot(a, b, preferred_element_type=F32)


def vmem():
    return pl.BlockSpec(memory_space=pltpu.VMEM)


def smem():
    return pl.BlockSpec(memory_space=pltpu.SMEM)


def moments_kernel(x_ref, basis_ref, links_ref, out_ref):
    links = links_ref[...].reshape(2, 64, 64)
    leaves = []
    for i in range(2):
        moment = lax.dot_general(
            x_ref[:, 256 * i : 256 * (i + 1)],
            basis_ref[i],
            (((1,), (1,)), ((), ())),
            preferred_element_type=F32,
        )
        leaves.append(moment.astype(BF16))
    parent = dot(leaves[0], links[0]) + dot(leaves[1], links[1])
    low = jnp.concatenate(leaves, axis=1)
    high = jnp.concatenate([parent[:16], parent[16:]], axis=1).astype(BF16)
    for r in range(out_ref.shape[0]):
        out_ref[r, 0:32, :] = low
        out_ref[r, 32:48, :] = high


def beside(matrices):
    half = matrices.shape[0] // 2
    return jnp.concatenate([matrices[:half], matrices[half:]], axis=2)


def matrix(ref, j):
    side, place = divmod(j, ref.shape[0])
    return ref[place, :, 64 * side : 64 * (side + 1)]


def prepare_kernel(
    coupling_in, top_in, links_in, rows_in, cols_in, near_in, x_in, near_rows_in, near_cols_in,
    blocks_ref, up_ref, down_ref, rows_ref, cols_ref, nearby_ref,
    coupling_ref, top_ref, links_ref, near_ref, x_ref, near_rows_ref, near_cols_ref, sems,
):
    pairs = (
        (links_in.at[0], links_ref),
        (top_in.at[0], top_ref),
        (coupling_in, coupling_ref),
        (near_rows_in, near_rows_ref),
        (near_cols_in, near_cols_ref),
        (x_in, x_ref),
        (near_in, near_ref),
        (rows_in, rows_ref),
        (cols_in, cols_ref),
    )
    copies = [pltpu.make_async_copy(source, target, sems.at[i]) for i, (source, target) in enumerate(pairs)]
    for copy in copies:
        copy.start()
    copies[0].wait()
    links = links_ref[...].reshape(56, 64, 64)
    for b in range(16):
        one = jnp.concatenate([links[2 * b], links[2 * b + 1]], axis=1)
        two = dot(links[32 + b], one).astype(BF16)
        three = dot(links[48 + b // 2], two).astype(BF16)
        down_ref[b, 0:64, :] = one
        down_ref[b, 64:128, :] = two
        down_ref[b, 128:192, :] = three
    copies[1].wait()
    up_ref[...] = beside(top_ref[...].reshape(48, 64, 64))
    copies[2].wait()
    blocks_ref[...] = beside(coupling_ref[...].reshape(128, 64, 64))
    for copy in copies[3:7]:
        copy.wait()
    nearby_ref[...] = jnp.zeros_like(nearby_ref)
    for s in range(8):
        start = pl.multiple_of(near_cols_ref[s] * 256, 256)
        nearby_ref[near_rows_ref[s]] += dot(x_ref[:, pl.ds(start, 256)], near_ref[s])
    for copy in copies[7:]:
        copy.wait()


def tree_kernel(
    rows_ref, cols_ref, got_ref, top_ref, coupling_ref, down_ref, out_ref,
    mom0, mom1, mom2, mom3, acc0, acc1, acc2, acc3,
):
    mom, acc = (mom0, mom1, mom2, mom3), (acc0, acc1, acc2, acc3)
    for a in range(32):
        parent = got_ref[a, 32:48, :]
        mom1[a, 0:16] = parent[:, 0:64]
        mom1[a, 16:32] = parent[:, 64:128]
    for p in range(16):
        mom2[p] = (dot(mom1[2 * p], matrix(top_ref, 2 * p)) + dot(mom1[2 * p + 1], matrix(top_ref, 2 * p + 1))).astype(BF16)
    for a in range(32):
        both = got_ref[a, 0:32, :]
        mom0[2 * a] = both[:, 0:64]
        mom0[2 * a + 1] = both[:, 64:128]
    for p in range(8):
        mom3[p] = (dot(mom2[2 * p], matrix(top_ref, 32 + 2 * p)) + dot(mom2[2 * p + 1], matrix(top_ref, 33 + 2 * p))).astype(BF16)
    for depth in range(4):
        acc[depth][...] = jnp.zeros_like(acc[depth])
    for s in range(32):
        for depth in range(4):
            q, p = cols_ref[depth, s], rows_ref[depth, s]
            acc[depth][p] += dot(mom[depth][q], matrix(coupling_ref, depth * 32 + s))
    for b in range(16):
        upper = jnp.concatenate([acc1[b], acc2[b // 2], acc3[b // 4]], axis=1).astype(BF16)
        own = jnp.concatenate([acc0[2 * b], acc0[2 * b + 1]], axis=1)
        out_ref[b] = (own + dot(upper, down_ref[b])).astype(BF16)


def output_kernel(got_ref, basis_ref, near_ref, out_ref):
    total = got_ref[0].astype(F32)
    for b in range(1, got_ref.shape[0]):
        total += got_ref[b].astype(F32)
    leaf_local = total.astype(BF16)
    for i in range(2):
        distant = dot(leaf_local[:, 64 * i : 64 * (i + 1)], basis_ref[i])
        out_ref[:, 256 * i : 256 * (i + 1)] = (distant + near_ref[i]).astype(BF16)


def local(
    columns_x,
    col_basis,
    col_links,
    col_top_links,
    row_basis,
    row_links,
    coupling,
    coupling_rows,
    coupling_cols,
    near_blocks,
    near_rows,
    near_cols,
):
    message = pl.pallas_call(
        moments_kernel,
        out_shape=jax.ShapeDtypeStruct((32, 48, 128), BF16),
        in_specs=[vmem()] * 3,
        out_specs=vmem(),
        name="moments",
    )(columns_x, col_basis, col_links)
    gathered = lax.all_to_all(message, "row", 0, 0)
    blocks, up, down, rows, cols, nearby = pl.pallas_call(
        prepare_kernel,
        out_shape=[
            pltpu.VMEM((64, 64, 128), BF16),
            pltpu.VMEM((24, 64, 128), BF16),
            pltpu.VMEM((16, 192, 128), BF16),
            pltpu.SMEM((4, 32), jnp.int32),
            pltpu.SMEM((4, 32), jnp.int32),
            pltpu.VMEM((2, 32, 256), F32),
        ],
        in_specs=[pl.BlockSpec(memory_space=pl.ANY)] * 9,
        out_specs=[vmem()] * 3 + [smem()] * 2 + [vmem()],
        scratch_shapes=[
            pltpu.VMEM((128, 4096), BF16),
            pltpu.VMEM((48, 4096), BF16),
            pltpu.VMEM((56, 4096), BF16),
            pltpu.VMEM((8, 256, 256), BF16),
            pltpu.VMEM((32, 512), BF16),
            pltpu.SMEM((8,), jnp.int32),
            pltpu.SMEM((8,), jnp.int32),
            pltpu.SemaphoreType.DMA((9,)),
        ],
        compiler_params=pltpu.CompilerParams(vmem_limit_bytes=60 * 1024 * 1024),
        cost_estimate=pl.CostEstimate(flops=33_554_432, bytes_accessed=8_000_000, transcendentals=0),
        name="prepare",
    )(
        coupling, col_top_links, row_links, coupling_rows, coupling_cols,
        near_blocks, columns_x, near_rows, near_cols,
    )
    gathered, nearby = lax.optimization_barrier((gathered, nearby))
    partials = pl.pallas_call(
        tree_kernel,
        out_shape=jax.ShapeDtypeStruct((16, 32, 128), BF16),
        in_specs=[smem()] * 2 + [vmem()] * 4,
        out_specs=vmem(),
        scratch_shapes=[pltpu.VMEM((64 >> depth, 32, 64), BF16) for depth in range(4)]
        + [pltpu.VMEM((32 >> depth, 32, 64), F32) for depth in range(4)],
        compiler_params=pltpu.CompilerParams(vmem_limit_bytes=16 * 1024 * 1024),
        name="trees",
    )(rows, cols, gathered, up, blocks, down)
    scattered = lax.all_to_all(partials, "col", 0, 0)
    return pl.pallas_call(
        output_kernel,
        out_shape=jax.ShapeDtypeStruct((32, 512), BF16),
        in_specs=[vmem()] * 3,
        out_specs=vmem(),
        compiler_params=pltpu.CompilerParams(vmem_limit_bytes=8 * 1024 * 1024),
        name="outputs",
    )(scattered, row_basis, nearby)


def solution(mesh):
    in_specs = (
        P(None, ("row", "col")),
        P(("row", "col"), None, None),
        P(("row", "col"), None),
        P("col", None, None),
        P(("row", "col"), None, None),
        P("row", None, None),
        P(("row", "col"), None),
        P(("row", "col"), None),
        P(("row", "col"), None),
        P(("row", "col"), None, None),
        P(("row", "col")),
        P(("row", "col")),
    )
    out_specs = P(None, ("row", "col"))
    return jax.shard_map(local, mesh=mesh, in_specs=in_specs, out_specs=out_specs, check_vma=False)
```

```python
import jax
import jax.numpy as jnp
from jax import lax
from jax.experimental import pallas as pl
from jax.experimental.pallas import tpu as pltpu
from jax.sharding import PartitionSpec as P

ROW_ORDER = [(20 + j) % 32 for j in range(32)]
COL_ORDER = [(8 + j) % 16 for j in range(16)]

F32 = jnp.float32
BF16 = jnp.bfloat16


def dot(a, b):
    return jnp.dot(a, b, preferred_element_type=F32)


def vmem():
    return pl.BlockSpec(memory_space=pltpu.VMEM)


def smem():
    return pl.BlockSpec(memory_space=pltpu.SMEM)


def moments_kernel(x_ref, basis_ref, links_ref, out_ref):
    links = links_ref[...].reshape(2, 64, 64)
    leaves = []
    for i in range(2):
        moment = lax.dot_general(
            x_ref[:, 256 * i : 256 * (i + 1)],
            basis_ref[i],
            (((1,), (1,)), ((), ())),
            preferred_element_type=F32,
        )
        leaves.append(moment.astype(BF16))
    parent = dot(leaves[0], links[0]) + dot(leaves[1], links[1])
    low = jnp.concatenate(leaves, axis=1)
    high = jnp.concatenate([parent[:16], parent[16:]], axis=1).astype(BF16)
    for r in range(out_ref.shape[0]):
        out_ref[r, 0:32, :] = low
        out_ref[r, 32:48, :] = high


def beside(matrices):
    half = matrices.shape[0] // 2
    return jnp.concatenate([matrices[:half], matrices[half:]], axis=2)


def matrix(ref, j):
    side, place = divmod(j, ref.shape[0])
    return ref[place, :, 64 * side : 64 * (side + 1)]


def prepare_kernel(
    coupling_in, top_in, links_in, rows_in, cols_in, near_in, x_in, near_rows_in, near_cols_in,
    blocks_ref, up_ref, down_ref, rows_ref, cols_ref, nearby_ref,
    coupling_ref, top_ref, links_ref, near_ref, x_ref, near_rows_ref, near_cols_ref, sems,
):
    pairs = (
        (links_in.at[0], links_ref),
        (top_in.at[0], top_ref),
        (coupling_in, coupling_ref),
        (near_rows_in, near_rows_ref),
        (near_cols_in, near_cols_ref),
        (x_in, x_ref),
        (near_in, near_ref),
        (rows_in, rows_ref),
        (cols_in, cols_ref),
    )
    copies = [pltpu.make_async_copy(source, target, sems.at[i]) for i, (source, target) in enumerate(pairs)]
    for copy in copies:
        copy.start()
    copies[0].wait()
    links = links_ref[...].reshape(56, 64, 64)
    for b in range(16):
        one = jnp.concatenate([links[2 * b], links[2 * b + 1]], axis=1)
        two = dot(links[32 + b], one).astype(BF16)
        three = dot(links[48 + b // 2], two).astype(BF16)
        down_ref[b, 0:64, :] = one
        down_ref[b, 64:128, :] = two
        down_ref[b, 128:192, :] = three
    copies[1].wait()
    up_ref[...] = beside(top_ref[...].reshape(48, 64, 64))
    copies[2].wait()
    blocks_ref[...] = beside(coupling_ref[...].reshape(128, 64, 64))
    for copy in copies[3:7]:
        copy.wait()
    nearby_ref[...] = jnp.zeros_like(nearby_ref)
    for s in range(8):
        start = pl.multiple_of(near_cols_ref[s] * 256, 256)
        nearby_ref[near_rows_ref[s]] += dot(x_ref[:, pl.ds(start, 256)], near_ref[s])
    for copy in copies[7:]:
        copy.wait()


def tree_kernel(
    rows_ref, cols_ref, got_ref, top_ref, coupling_ref, down_ref, out_ref,
    mom0, mom1, mom2, mom3, acc0, acc1, acc2, acc3,
):
    mom, acc = (mom0, mom1, mom2, mom3), (acc0, acc1, acc2, acc3)
    for j, a in enumerate(ROW_ORDER):
        parent = got_ref[j, 32:48, :]
        mom1[a, 0:16] = parent[:, 0:64]
        mom1[a, 16:32] = parent[:, 64:128]
    for p in range(16):
        mom2[p] = (dot(mom1[2 * p], matrix(top_ref, 2 * p)) + dot(mom1[2 * p + 1], matrix(top_ref, 2 * p + 1))).astype(BF16)
    for j, a in enumerate(ROW_ORDER):
        both = got_ref[j, 0:32, :]
        mom0[2 * a] = both[:, 0:64]
        mom0[2 * a + 1] = both[:, 64:128]
    for p in range(8):
        mom3[p] = (dot(mom2[2 * p], matrix(top_ref, 32 + 2 * p)) + dot(mom2[2 * p + 1], matrix(top_ref, 33 + 2 * p))).astype(BF16)
    for depth in range(4):
        acc[depth][...] = jnp.zeros_like(acc[depth])
    for s in range(32):
        for depth in range(4):
            q, p = cols_ref[depth, s], rows_ref[depth, s]
            acc[depth][p] += dot(mom[depth][q], matrix(coupling_ref, depth * 32 + s))
    for j, b in enumerate(COL_ORDER):
        upper = jnp.concatenate([acc1[b], acc2[b // 2], acc3[b // 4]], axis=1).astype(BF16)
        own = jnp.concatenate([acc0[2 * b], acc0[2 * b + 1]], axis=1)
        out_ref[j] = (own + dot(upper, down_ref[b])).astype(BF16)


def output_kernel(got_ref, basis_ref, near_ref, out_ref):
    total = got_ref[0].astype(F32)
    for b in range(1, got_ref.shape[0]):
        total += got_ref[b].astype(F32)
    leaf_local = total.astype(BF16)
    for i in range(2):
        distant = dot(leaf_local[:, 64 * i : 64 * (i + 1)], basis_ref[i])
        out_ref[:, 256 * i : 256 * (i + 1)] = (distant + near_ref[i]).astype(BF16)


def local(
    columns_x,
    col_basis,
    col_links,
    col_top_links,
    row_basis,
    row_links,
    coupling,
    coupling_rows,
    coupling_cols,
    near_blocks,
    near_rows,
    near_cols,
):
    message = pl.pallas_call(
        moments_kernel,
        out_shape=jax.ShapeDtypeStruct((32, 48, 128), BF16),
        in_specs=[vmem()] * 3,
        out_specs=vmem(),
        name="moments",
    )(columns_x, col_basis, col_links)
    gathered = lax.all_to_all(message, "row", 0, 0, axis_index_groups=[ROW_ORDER])
    blocks, up, down, rows, cols, nearby = pl.pallas_call(
        prepare_kernel,
        out_shape=[
            pltpu.VMEM((64, 64, 128), BF16),
            pltpu.VMEM((24, 64, 128), BF16),
            pltpu.VMEM((16, 192, 128), BF16),
            pltpu.SMEM((4, 32), jnp.int32),
            pltpu.SMEM((4, 32), jnp.int32),
            pltpu.VMEM((2, 32, 256), F32),
        ],
        in_specs=[pl.BlockSpec(memory_space=pl.ANY)] * 9,
        out_specs=[vmem()] * 3 + [smem()] * 2 + [vmem()],
        scratch_shapes=[
            pltpu.VMEM((128, 4096), BF16),
            pltpu.VMEM((48, 4096), BF16),
            pltpu.VMEM((56, 4096), BF16),
            pltpu.VMEM((8, 256, 256), BF16),
            pltpu.VMEM((32, 512), BF16),
            pltpu.SMEM((8,), jnp.int32),
            pltpu.SMEM((8,), jnp.int32),
            pltpu.SemaphoreType.DMA((9,)),
        ],
        compiler_params=pltpu.CompilerParams(vmem_limit_bytes=60 * 1024 * 1024),
        cost_estimate=pl.CostEstimate(flops=33_554_432, bytes_accessed=8_000_000, transcendentals=0),
        name="prepare",
    )(
        coupling, col_top_links, row_links, coupling_rows, coupling_cols,
        near_blocks, columns_x, near_rows, near_cols,
    )
    gathered, nearby = lax.optimization_barrier((gathered, nearby))
    partials = pl.pallas_call(
        tree_kernel,
        out_shape=jax.ShapeDtypeStruct((16, 32, 128), BF16),
        in_specs=[smem()] * 2 + [vmem()] * 4,
        out_specs=vmem(),
        scratch_shapes=[pltpu.VMEM((64 >> depth, 32, 64), BF16) for depth in range(4)]
        + [pltpu.VMEM((32 >> depth, 32, 64), F32) for depth in range(4)],
        compiler_params=pltpu.CompilerParams(vmem_limit_bytes=16 * 1024 * 1024),
        name="trees",
    )(rows, cols, gathered, up, blocks, down)
    scattered = lax.all_to_all(partials, "col", 0, 0, axis_index_groups=[COL_ORDER])
    return pl.pallas_call(
        output_kernel,
        out_shape=jax.ShapeDtypeStruct((32, 512), BF16),
        in_specs=[vmem()] * 3,
        out_specs=vmem(),
        compiler_params=pltpu.CompilerParams(vmem_limit_bytes=8 * 1024 * 1024),
        name="outputs",
    )(scattered, row_basis, nearby)


def solution(mesh):
    in_specs = (
        P(None, ("row", "col")),
        P(("row", "col"), None, None),
        P(("row", "col"), None),
        P("col", None, None),
        P(("row", "col"), None, None),
        P("row", None, None),
        P(("row", "col"), None),
        P(("row", "col"), None),
        P(("row", "col"), None),
        P(("row", "col"), None, None),
        P(("row", "col")),
        P(("row", "col")),
    )
    out_specs = P(None, ("row", "col"))
    return jax.shard_map(local, mesh=mesh, in_specs=in_specs, out_specs=out_specs, check_vma=False)
```

```python
import jax
import jax.numpy as jnp
from jax import lax
from jax.experimental import pallas as pl
from jax.experimental.pallas import tpu as pltpu
from jax.sharding import PartitionSpec as P

CHIP_ORDER = [(10 + j) % 16 for j in range(16)]
COL_ORDER = [(8 + j) % 16 for j in range(16)]

F32 = jnp.float32
BF16 = jnp.bfloat16


def dot(a, b):
    return jnp.dot(a, b, preferred_element_type=F32)


def vmem():
    return pl.BlockSpec(memory_space=pltpu.VMEM)


def smem():
    return pl.BlockSpec(memory_space=pltpu.SMEM)


def moments_kernel(x_ref, basis_ref, links_ref, out_ref):
    links = links_ref[...].reshape(2, 64, 64)
    leaves = []
    for i in range(2):
        moment = lax.dot_general(
            x_ref[:, 256 * i : 256 * (i + 1)],
            basis_ref[i],
            (((1,), (1,)), ((), ())),
            preferred_element_type=F32,
        )
        leaves.append(moment.astype(BF16))
    parent = dot(leaves[0], links[0]) + dot(leaves[1], links[1])
    low = jnp.concatenate(leaves, axis=1)
    high = jnp.concatenate([parent[:16], parent[16:]], axis=1).astype(BF16)
    for r in range(out_ref.shape[0]):
        out_ref[r, 0:32, :] = low
        out_ref[r, 32:48, :] = high


def beside(matrices):
    half = matrices.shape[0] // 2
    return jnp.concatenate([matrices[:half], matrices[half:]], axis=2)


def matrix(ref, j):
    side, place = divmod(j, ref.shape[0])
    return ref[place, :, 64 * side : 64 * (side + 1)]


def prepare_kernel(
    coupling_in, top_in, links_in, rows_in, cols_in, near_in, x_in, near_rows_in, near_cols_in,
    blocks_ref, up_ref, down_ref, rows_ref, cols_ref, nearby_ref,
    coupling_ref, top_ref, links_ref, near_ref, x_ref, near_rows_ref, near_cols_ref, sems,
):
    pairs = (
        (links_in.at[0], links_ref),
        (top_in.at[0], top_ref),
        (coupling_in, coupling_ref),
        (near_rows_in, near_rows_ref),
        (near_cols_in, near_cols_ref),
        (x_in, x_ref),
        (near_in, near_ref),
        (rows_in, rows_ref),
        (cols_in, cols_ref),
    )
    copies = [pltpu.make_async_copy(source, target, sems.at[i]) for i, (source, target) in enumerate(pairs)]
    for copy in copies:
        copy.start()
    copies[0].wait()
    links = links_ref[...].reshape(56, 64, 64)
    for b in range(16):
        one = jnp.concatenate([links[2 * b], links[2 * b + 1]], axis=1)
        two = dot(links[32 + b], one).astype(BF16)
        three = dot(links[48 + b // 2], two).astype(BF16)
        down_ref[b, 0:64, :] = one
        down_ref[b, 64:128, :] = two
        down_ref[b, 128:192, :] = three
    copies[1].wait()
    up_ref[...] = beside(top_ref[...].reshape(48, 64, 64))
    copies[2].wait()
    blocks_ref[...] = beside(coupling_ref[...].reshape(128, 64, 64))
    for copy in copies[3:7]:
        copy.wait()
    nearby_ref[...] = jnp.zeros_like(nearby_ref)
    for s in range(8):
        start = pl.multiple_of(near_cols_ref[s] * 256, 256)
        nearby_ref[near_rows_ref[s]] += dot(x_ref[:, pl.ds(start, 256)], near_ref[s])
    for copy in copies[7:]:
        copy.wait()


def tree_kernel(
    rows_ref, cols_ref, got_ref, top_ref, coupling_ref, down_ref, out_ref,
    mom0, mom1, mom2, mom3, acc0, acc1, acc2, acc3,
):
    mom, acc = (mom0, mom1, mom2, mom3), (acc0, acc1, acc2, acc3)
    received = [(2 * chip + core, core, j) for j, chip in enumerate(CHIP_ORDER) for core in range(2)]
    for a, core, j in received:
        parent = got_ref[core, j, 32:48, :]
        mom1[a, 0:16] = parent[:, 0:64]
        mom1[a, 16:32] = parent[:, 64:128]
    for p in range(16):
        mom2[p] = (dot(mom1[2 * p], matrix(top_ref, 2 * p)) + dot(mom1[2 * p + 1], matrix(top_ref, 2 * p + 1))).astype(BF16)
    for a, core, j in received:
        both = got_ref[core, j, 0:32, :]
        mom0[2 * a] = both[:, 0:64]
        mom0[2 * a + 1] = both[:, 64:128]
    for p in range(8):
        mom3[p] = (dot(mom2[2 * p], matrix(top_ref, 32 + 2 * p)) + dot(mom2[2 * p + 1], matrix(top_ref, 33 + 2 * p))).astype(BF16)
    for depth in range(4):
        acc[depth][...] = jnp.zeros_like(acc[depth])
    for s in range(32):
        for depth in (0, 1):
            first, second = cols_ref[depth, s], cols_ref[depth + 2, s]
            picked = jnp.concatenate([mom[depth][first], mom[depth + 2][second]], axis=0)
            term = dot(picked, coupling_ref[depth * 32 + s])
            acc[depth][rows_ref[depth, s]] += term[0:32, 0:64]
            acc[depth + 2][rows_ref[depth + 2, s], :, 64:128] += term[32:64, 64:128]
    for j, b in enumerate(COL_ORDER):
        upper = jnp.concatenate([acc1[b], acc2[b // 2, :, 64:128], acc3[b // 4, :, 64:128]], axis=1).astype(BF16)
        own = jnp.concatenate([acc0[2 * b], acc0[2 * b + 1]], axis=1)
        out_ref[j] = (own + dot(upper, down_ref[b])).astype(BF16)


def output_kernel(got_ref, basis_ref, near_ref, out_ref):
    total = got_ref[0].astype(F32)
    for b in range(1, got_ref.shape[0]):
        total += got_ref[b].astype(F32)
    leaf_local = total.astype(BF16)
    for i in range(2):
        distant = dot(leaf_local[:, 64 * i : 64 * (i + 1)], basis_ref[i])
        out_ref[:, 256 * i : 256 * (i + 1)] = (distant + near_ref[i]).astype(BF16)


def local(
    columns_x,
    col_basis,
    col_links,
    col_top_links,
    row_basis,
    row_links,
    coupling,
    coupling_rows,
    coupling_cols,
    near_blocks,
    near_rows,
    near_cols,
):
    message = pl.pallas_call(
        moments_kernel,
        out_shape=jax.ShapeDtypeStruct((16, 48, 128), BF16),
        in_specs=[vmem()] * 3,
        out_specs=vmem(),
        name="moments",
    )(columns_x, col_basis, col_links)
    same_core = [[2 * chip + core for chip in CHIP_ORDER] for core in range(2)]
    same_chip = [[2 * chip, 2 * chip + 1] for chip in range(16)]
    arrived = lax.all_to_all(message, "row", 0, 0, axis_index_groups=same_core)
    blocks, up, down, rows, cols, nearby = pl.pallas_call(
        prepare_kernel,
        out_shape=[
            pltpu.VMEM((64, 64, 128), BF16),
            pltpu.VMEM((24, 64, 128), BF16),
            pltpu.VMEM((16, 192, 128), BF16),
            pltpu.SMEM((4, 32), jnp.int32),
            pltpu.SMEM((4, 32), jnp.int32),
            pltpu.VMEM((2, 32, 256), F32),
        ],
        in_specs=[pl.BlockSpec(memory_space=pl.ANY)] * 9,
        out_specs=[vmem()] * 3 + [smem()] * 2 + [vmem()],
        scratch_shapes=[
            pltpu.VMEM((128, 4096), BF16),
            pltpu.VMEM((48, 4096), BF16),
            pltpu.VMEM((56, 4096), BF16),
            pltpu.VMEM((8, 256, 256), BF16),
            pltpu.VMEM((32, 512), BF16),
            pltpu.SMEM((8,), jnp.int32),
            pltpu.SMEM((8,), jnp.int32),
            pltpu.SemaphoreType.DMA((9,)),
        ],
        compiler_params=pltpu.CompilerParams(vmem_limit_bytes=60 * 1024 * 1024),
        cost_estimate=pl.CostEstimate(flops=33_554_432, bytes_accessed=8_000_000, transcendentals=0),
        name="prepare",
    )(
        coupling, col_top_links, row_links, coupling_rows, coupling_cols,
        near_blocks, columns_x, near_rows, near_cols,
    )
    arrived, nearby = lax.optimization_barrier((arrived, nearby))
    gathered = lax.all_gather(arrived, "row", axis=0, axis_index_groups=same_chip)
    partials = pl.pallas_call(
        tree_kernel,
        out_shape=jax.ShapeDtypeStruct((16, 32, 128), BF16),
        in_specs=[smem()] * 2 + [vmem()] * 4,
        out_specs=vmem(),
        scratch_shapes=[pltpu.VMEM((64 >> depth, 32, 64), BF16) for depth in range(4)]
        + [pltpu.VMEM((32 >> depth, 32, 64 if depth < 2 else 128), F32) for depth in range(4)],
        compiler_params=pltpu.CompilerParams(vmem_limit_bytes=16 * 1024 * 1024),
        name="trees",
    )(rows, cols, gathered, up, blocks, down)
    scattered = lax.all_to_all(partials, "col", 0, 0, axis_index_groups=[COL_ORDER])
    return pl.pallas_call(
        output_kernel,
        out_shape=jax.ShapeDtypeStruct((32, 512), BF16),
        in_specs=[vmem()] * 3,
        out_specs=vmem(),
        compiler_params=pltpu.CompilerParams(vmem_limit_bytes=8 * 1024 * 1024),
        name="outputs",
    )(scattered, row_basis, nearby)


def solution(mesh):
    in_specs = (
        P(None, ("row", "col")),
        P(("row", "col"), None, None),
        P(("row", "col"), None),
        P("col", None, None),
        P(("row", "col"), None, None),
        P("row", None, None),
        P(("row", "col"), None),
        P(("row", "col"), None),
        P(("row", "col"), None),
        P(("row", "col"), None, None),
        P(("row", "col")),
        P(("row", "col")),
    )
    out_specs = P(None, ("row", "col"))
    return jax.shard_map(local, mesh=mesh, in_specs=in_specs, out_specs=out_specs, check_vma=False)
```

```python
import jax
import jax.numpy as jnp
from jax import lax
from jax.experimental import pallas as pl
from jax.experimental.pallas import tpu as pltpu
from jax.sharding import PartitionSpec as P

CHIP_ORDER = [(10 + j) % 16 for j in range(16)]
COL_ORDER = [(8 + 7 * j) % 16 for j in range(16)]

F32 = jnp.float32
BF16 = jnp.bfloat16


def dot(a, b):
    return jnp.dot(a, b, preferred_element_type=F32)


def vmem():
    return pl.BlockSpec(memory_space=pltpu.VMEM)


def smem():
    return pl.BlockSpec(memory_space=pltpu.SMEM)


def moments_kernel(x_ref, basis_ref, links_ref, out_ref):
    links = links_ref[...].reshape(2, 64, 64)
    leaves = []
    for i in range(2):
        moment = lax.dot_general(
            x_ref[:, 256 * i : 256 * (i + 1)],
            basis_ref[i],
            (((1,), (1,)), ((), ())),
            preferred_element_type=F32,
        )
        leaves.append(moment.astype(BF16))
    parent = dot(leaves[0], links[0]) + dot(leaves[1], links[1])
    low = jnp.concatenate(leaves, axis=1)
    high = jnp.concatenate([parent[:16], parent[16:]], axis=1).astype(BF16)
    for r in range(out_ref.shape[0]):
        out_ref[r, 0:32, :] = low
        out_ref[r, 32:48, :] = high


def beside(matrices):
    half = matrices.shape[0] // 2
    return jnp.concatenate([matrices[:half], matrices[half:]], axis=2)


def paired(first, second):
    columns = []
    for i in range(0, first.shape[1], 128):
        one, two = first[:, i : i + 128], second[:, i : i + 128]
        columns.append(jnp.concatenate([one[:, 0:64], two[:, 0:64]], axis=1))
        columns.append(jnp.concatenate([one[:, 64:128], two[:, 64:128]], axis=1))
    return jnp.concatenate(columns, axis=1).reshape(first.shape[0], 64, 128)


def matrix(ref, j):
    side, place = divmod(j, ref.shape[0])
    return ref[place, :, 64 * side : 64 * (side + 1)]


def prepare_kernel(
    coupling_in, top_in, links_in, rows_in, cols_in, near_in, x_in, near_rows_in, near_cols_in,
    blocks_ref, up_ref, down_ref, rows_ref, cols_ref, nearby_ref,
    coupling_ref, top_ref, links_ref, near_ref, x_ref, near_rows_ref, near_cols_ref, sems,
):
    pairs = (
        (links_in.at[0], links_ref),
        (top_in.at[0], top_ref),
        (coupling_in, coupling_ref),
        (near_rows_in, near_rows_ref),
        (near_cols_in, near_cols_ref),
        (x_in, x_ref),
        (near_in, near_ref),
        (rows_in, rows_ref),
        (cols_in, cols_ref),
    )
    copies = [pltpu.make_async_copy(source, target, sems.at[i]) for i, (source, target) in enumerate(pairs)]
    for copy in copies:
        copy.start()
    copies[0].wait()
    links = links_ref[...].reshape(56, 64, 64)
    for b in range(16):
        one = jnp.concatenate([links[2 * b], links[2 * b + 1]], axis=1)
        two = dot(links[32 + b], one).astype(BF16)
        three = dot(links[48 + b // 2], two).astype(BF16)
        down_ref[b, 0:64, :] = one
        down_ref[b, 64:128, :] = two
        down_ref[b, 128:192, :] = three
    copies[1].wait()
    up_ref[...] = beside(top_ref[...].reshape(48, 64, 64))
    copies[2].wait()
    for i in range(0, 64, 16):
        blocks_ref[i : i + 16] = paired(coupling_ref[i : i + 16], coupling_ref[64 + i : 80 + i])
    for copy in copies[3:7]:
        copy.wait()
    nearby_ref[...] = jnp.zeros_like(nearby_ref)
    for s in range(8):
        start = pl.multiple_of(near_cols_ref[s] * 256, 256)
        nearby_ref[near_rows_ref[s]] += dot(x_ref[:, pl.ds(start, 256)], near_ref[s])
    for copy in copies[7:]:
        copy.wait()


def tree_kernel(
    rows_ref, cols_ref, got_ref, top_ref, coupling_ref, down_ref, out_ref,
    mom0, mom1, mom2, mom3, acc0, acc1, acc2, acc3,
):
    mom, acc = (mom0, mom1, mom2, mom3), (acc0, acc1, acc2, acc3)
    received = [(2 * chip + core, core, j) for j, chip in enumerate(CHIP_ORDER) for core in range(2)]
    for a, core, j in received:
        parent = got_ref[core, j, 32:48, :]
        mom1[a, 0:16] = parent[:, 0:64]
        mom1[a, 16:32] = parent[:, 64:128]
    for p in range(16):
        mom2[p] = (dot(mom1[2 * p], matrix(top_ref, 2 * p)) + dot(mom1[2 * p + 1], matrix(top_ref, 2 * p + 1))).astype(BF16)
    for a, core, j in received:
        both = got_ref[core, j, 0:32, :]
        mom0[2 * a] = both[:, 0:64]
        mom0[2 * a + 1] = both[:, 64:128]
    for p in range(8):
        mom3[p] = (dot(mom2[2 * p], matrix(top_ref, 32 + 2 * p)) + dot(mom2[2 * p + 1], matrix(top_ref, 33 + 2 * p))).astype(BF16)
    for depth in range(4):
        acc[depth][...] = jnp.zeros_like(acc[depth])
    for s in range(32):
        for depth in (0, 1):
            first, second = cols_ref[depth, s], cols_ref[depth + 2, s]
            picked = jnp.concatenate([mom[depth][first], mom[depth + 2][second]], axis=0)
            term = dot(picked, coupling_ref[depth * 32 + s])
            acc[depth][rows_ref[depth, s]] += term[0:32, 0:64]
            acc[depth + 2][rows_ref[depth + 2, s], :, 64:128] += term[32:64, 64:128]
    for j, b in enumerate(COL_ORDER):
        upper = jnp.concatenate([acc1[b], acc2[b // 2, :, 64:128], acc3[b // 4, :, 64:128]], axis=1).astype(BF16)
        own = jnp.concatenate([acc0[2 * b], acc0[2 * b + 1]], axis=1)
        out_ref[j] = (own + dot(upper, down_ref[b])).astype(BF16)


def output_kernel(got_ref, basis_ref, near_ref, out_ref):
    total = got_ref[0].astype(F32)
    for b in range(1, got_ref.shape[0]):
        total += got_ref[b].astype(F32)
    leaf_local = total.astype(BF16)
    for i in range(2):
        distant = dot(leaf_local[:, 64 * i : 64 * (i + 1)], basis_ref[i])
        out_ref[:, 256 * i : 256 * (i + 1)] = (distant + near_ref[i]).astype(BF16)


def local(
    columns_x,
    col_basis,
    col_links,
    col_top_links,
    row_basis,
    row_links,
    coupling,
    coupling_rows,
    coupling_cols,
    near_blocks,
    near_rows,
    near_cols,
):
    message = pl.pallas_call(
        moments_kernel,
        out_shape=jax.ShapeDtypeStruct((16, 48, 128), BF16),
        in_specs=[vmem()] * 3,
        out_specs=vmem(),
        name="moments",
    )(columns_x, col_basis, col_links)
    same_core = [[2 * chip + core for chip in CHIP_ORDER] for core in range(2)]
    same_chip = [[2 * chip, 2 * chip + 1] for chip in range(16)]
    arrived = lax.all_to_all(message, "row", 0, 0, axis_index_groups=same_core)
    blocks, up, down, rows, cols, nearby = pl.pallas_call(
        prepare_kernel,
        out_shape=[
            pltpu.VMEM((64, 64, 128), BF16),
            pltpu.VMEM((24, 64, 128), BF16),
            pltpu.VMEM((16, 192, 128), BF16),
            pltpu.SMEM((4, 32), jnp.int32),
            pltpu.SMEM((4, 32), jnp.int32),
            pltpu.VMEM((2, 32, 256), F32),
        ],
        in_specs=[pl.BlockSpec(memory_space=pl.ANY)] * 9,
        out_specs=[vmem()] * 3 + [smem()] * 2 + [vmem()],
        scratch_shapes=[
            pltpu.VMEM((128, 4096), BF16),
            pltpu.VMEM((48, 4096), BF16),
            pltpu.VMEM((56, 4096), BF16),
            pltpu.VMEM((8, 256, 256), BF16),
            pltpu.VMEM((32, 512), BF16),
            pltpu.SMEM((8,), jnp.int32),
            pltpu.SMEM((8,), jnp.int32),
            pltpu.SemaphoreType.DMA((9,)),
        ],
        compiler_params=pltpu.CompilerParams(vmem_limit_bytes=60 * 1024 * 1024),
        cost_estimate=pl.CostEstimate(flops=33_554_432, bytes_accessed=8_000_000, transcendentals=0),
        name="prepare",
    )(
        coupling, col_top_links, row_links, coupling_rows, coupling_cols,
        near_blocks, columns_x, near_rows, near_cols,
    )
    arrived, nearby = lax.optimization_barrier((arrived, nearby))
    gathered = lax.all_gather(arrived, "row", axis=0, axis_index_groups=same_chip)
    partials = pl.pallas_call(
        tree_kernel,
        out_shape=jax.ShapeDtypeStruct((16, 32, 128), BF16),
        in_specs=[smem()] * 2 + [vmem()] * 4,
        out_specs=vmem(),
        scratch_shapes=[pltpu.VMEM((64 >> depth, 32, 64), BF16) for depth in range(4)]
        + [pltpu.VMEM((32 >> depth, 32, 64 if depth < 2 else 128), F32) for depth in range(4)],
        compiler_params=pltpu.CompilerParams(vmem_limit_bytes=16 * 1024 * 1024),
        name="trees",
    )(rows, cols, gathered, up, blocks, down)
    scattered = lax.all_to_all(partials, "col", 0, 0, axis_index_groups=[COL_ORDER])
    return pl.pallas_call(
        output_kernel,
        out_shape=jax.ShapeDtypeStruct((32, 512), BF16),
        in_specs=[vmem()] * 3,
        out_specs=vmem(),
        compiler_params=pltpu.CompilerParams(vmem_limit_bytes=8 * 1024 * 1024),
        name="outputs",
    )(scattered, row_basis, nearby)


def solution(mesh):
    in_specs = (
        P(None, ("row", "col")),
        P(("row", "col"), None, None),
        P(("row", "col"), None),
        P("col", None, None),
        P(("row", "col"), None, None),
        P("row", None, None),
        P(("row", "col"), None),
        P(("row", "col"), None),
        P(("row", "col"), None),
        P(("row", "col"), None, None),
        P(("row", "col")),
        P(("row", "col")),
    )
    out_specs = P(None, ("row", "col"))
    return jax.shard_map(local, mesh=mesh, in_specs=in_specs, out_specs=out_specs, check_vma=False)
```

```python
import jax
import jax.numpy as jnp
from jax import lax
from jax.experimental import pallas as pl
from jax.experimental.pallas import tpu as pltpu
from jax.sharding import PartitionSpec as P

CHIP_ORDER = [(10 + j) % 16 for j in range(16)]
COL_ORDER = [(11 + j) % 16 for j in range(16)]

F32 = jnp.float32
BF16 = jnp.bfloat16


def dot(a, b):
    return jnp.dot(a, b, preferred_element_type=F32)


def vmem():
    return pl.BlockSpec(memory_space=pltpu.VMEM)


def smem():
    return pl.BlockSpec(memory_space=pltpu.SMEM)


def moments_kernel(x_ref, basis_ref, links_ref, out_ref):
    links = links_ref[...].reshape(2, 64, 64)
    leaves = []
    for i in range(2):
        moment = lax.dot_general(
            x_ref[:, 256 * i : 256 * (i + 1)],
            basis_ref[i],
            (((1,), (1,)), ((), ())),
            preferred_element_type=F32,
        )
        leaves.append(moment.astype(BF16))
    parent = dot(leaves[0], links[0]) + dot(leaves[1], links[1])
    low = jnp.concatenate(leaves, axis=1)
    high = jnp.concatenate([parent[:16], parent[16:]], axis=1).astype(BF16)
    for r in range(out_ref.shape[0]):
        out_ref[r, 0:32, :] = low
        out_ref[r, 32:48, :] = high


def paired(first, second):
    columns = []
    for i in range(0, first.shape[1], 128):
        one, two = first[:, i : i + 128], second[:, i : i + 128]
        columns.append(jnp.concatenate([one[:, 0:64], two[:, 0:64]], axis=1))
        columns.append(jnp.concatenate([one[:, 64:128], two[:, 64:128]], axis=1))
    return jnp.concatenate(columns, axis=1).reshape(first.shape[0], 64, 128)


def prepare_kernel(
    coupling_in, top_in, links_in, rows_in, cols_in, near_in, x_in, near_rows_in, near_cols_in,
    blocks_ref, up_ref, down_ref, rows_ref, cols_ref, nearby_ref,
    coupling_ref, top_ref, links_ref, near_ref, x_ref, near_rows_ref, near_cols_ref, sems,
):
    pairs = (
        (links_in.at[0], links_ref),
        (top_in.at[0], top_ref),
        (coupling_in, coupling_ref),
        (near_rows_in, near_rows_ref),
        (near_cols_in, near_cols_ref),
        (x_in, x_ref),
        (near_in, near_ref),
        (rows_in, rows_ref),
        (cols_in, cols_ref),
    )
    copies = [pltpu.make_async_copy(source, target, sems.at[i]) for i, (source, target) in enumerate(pairs)]
    for copy in copies:
        copy.start()
    copies[0].wait()
    links = links_ref[...].reshape(56, 64, 64)
    for b in range(16):
        one = jnp.concatenate([links[2 * b], links[2 * b + 1]], axis=1)
        two = dot(links[32 + b], one).astype(BF16)
        three = dot(links[48 + b // 2], two).astype(BF16)
        down_ref[b, 0:64, :] = two
        down_ref[b, 64:128, :] = one
        down_ref[b, 128:192, :] = jnp.zeros_like(one)
        down_ref[b, 192:256, :] = three
    copies[1].wait()
    top = top_ref[...].reshape(48, 64, 64)
    for p in range(24):
        up_ref[p] = jnp.concatenate([top[2 * p], top[2 * p + 1]], axis=1)
    copies[2].wait()
    for place, i in ((0, 0), (16, 16), (32, 64), (48, 80)):
        blocks_ref[place : place + 16] = paired(coupling_ref[i : i + 16], coupling_ref[i + 32 : i + 48])
    for copy in copies[3:7]:
        copy.wait()
    nearby_ref[...] = jnp.zeros_like(nearby_ref)
    for s in range(8):
        start = pl.multiple_of(near_cols_ref[s] * 256, 256)
        nearby_ref[near_rows_ref[s]] += dot(x_ref[:, pl.ds(start, 256)], near_ref[s])
    for copy in copies[7:]:
        copy.wait()


def tree_kernel(
    rows_ref, cols_ref, got_ref, top_ref, coupling_ref, down_ref, out_ref,
    mom0, mom1, mom2, mom3, acc0, acc1, acc2, acc3,
):
    mom, acc = (mom0, mom1, mom2, mom3), (acc0, acc1, acc2, acc3)
    for depth in range(4):
        acc[depth][...] = jnp.zeros_like(acc[depth])
    received = [(2 * chip + core, core, j) for j, chip in enumerate(CHIP_ORDER) for core in range(2)]
    for a, core, j in received:
        parent = got_ref[core, j, 32:48, :]
        mom1[a, 0:16] = parent[:, 0:64]
        mom1[a, 16:32] = parent[:, 64:128]
    for p in range(16):
        both = dot(mom1[2 * p : 2 * p + 2].reshape(64, 64), top_ref[p])
        mom2[p] = (both[0:32, 0:64] + both[32:64, 64:128]).astype(BF16)
    for a, core, j in received:
        both = got_ref[core, j, 0:32, :]
        mom0[2 * a] = both[:, 0:64]
        mom0[2 * a + 1] = both[:, 64:128]
    for p in range(8):
        both = dot(mom2[2 * p : 2 * p + 2].reshape(64, 64), top_ref[16 + p])
        mom3[p] = (both[0:32, 0:64] + both[32:64, 64:128]).astype(BF16)
    for depth in (0, 2):
        for s in range(32):
            first, second = cols_ref[depth, s], cols_ref[depth + 1, s]
            picked = jnp.concatenate([mom[depth][first], mom[depth + 1][second]], axis=0)
            term = dot(picked, coupling_ref[depth * 16 + s])
            acc[depth][rows_ref[depth, s], :, 0:64] += term[0:32, 0:64]
            acc[depth + 1][rows_ref[depth + 1, s], :, 64:128] += term[32:64, 64:128]
    tops = [acc3[p].astype(BF16) for p in range(4)]
    for j, b in enumerate(COL_ORDER):
        upper = jnp.concatenate([(acc1[b] + acc2[b // 2]).astype(BF16), tops[b // 4]], axis=1)
        own = jnp.concatenate([acc0[2 * b], acc0[2 * b + 1]], axis=1)
        out_ref[j] = (own + dot(upper, down_ref[b])).astype(BF16)


def output_kernel(got_ref, basis_ref, near_ref, out_ref):
    total = got_ref[0].astype(F32)
    for b in range(1, got_ref.shape[0]):
        total += got_ref[b].astype(F32)
    leaf_local = total.astype(BF16)
    for i in range(2):
        distant = dot(leaf_local[:, 64 * i : 64 * (i + 1)], basis_ref[i])
        out_ref[:, 256 * i : 256 * (i + 1)] = (distant + near_ref[i]).astype(BF16)


def call_prepare(*operands):
    return pl.pallas_call(
        prepare_kernel,
        out_shape=[
            pltpu.VMEM((64, 64, 128), BF16),
            pltpu.VMEM((24, 64, 128), BF16),
            pltpu.VMEM((16, 256, 128), BF16),
            pltpu.SMEM((4, 32), jnp.int32),
            pltpu.SMEM((4, 32), jnp.int32),
            pltpu.VMEM((2, 32, 256), F32),
        ],
        in_specs=[pl.BlockSpec(memory_space=pl.ANY)] * 9,
        out_specs=[vmem()] * 3 + [smem()] * 2 + [vmem()],
        scratch_shapes=[
            pltpu.VMEM((128, 4096), BF16),
            pltpu.VMEM((48, 4096), BF16),
            pltpu.VMEM((56, 4096), BF16),
            pltpu.VMEM((8, 256, 256), BF16),
            pltpu.VMEM((32, 512), BF16),
            pltpu.SMEM((8,), jnp.int32),
            pltpu.SMEM((8,), jnp.int32),
            pltpu.SemaphoreType.DMA((9,)),
        ],
        compiler_params=pltpu.CompilerParams(vmem_limit_bytes=60 * 1024 * 1024),
        cost_estimate=pl.CostEstimate(flops=33_554_432, bytes_accessed=8_000_000, transcendentals=0),
        name="prepare",
    )(*operands)


def call_trees(*operands):
    return pl.pallas_call(
        tree_kernel,
        out_shape=jax.ShapeDtypeStruct((16, 32, 128), BF16),
        in_specs=[smem()] * 2 + [vmem()] * 4,
        out_specs=vmem(),
        scratch_shapes=[pltpu.VMEM((64 >> depth, 32, 64), BF16) for depth in range(4)]
        + [pltpu.VMEM((32 >> depth, 32, 128 if depth else 64), F32) for depth in range(4)],
        compiler_params=pltpu.CompilerParams(vmem_limit_bytes=16 * 1024 * 1024),
        name="trees",
    )(*operands)


def local(
    columns_x,
    col_basis,
    col_links,
    col_top_links,
    row_basis,
    row_links,
    coupling,
    coupling_rows,
    coupling_cols,
    near_blocks,
    near_rows,
    near_cols,
):
    message = pl.pallas_call(
        moments_kernel,
        out_shape=jax.ShapeDtypeStruct((16, 48, 128), BF16),
        in_specs=[vmem()] * 3,
        out_specs=vmem(),
        name="moments",
    )(columns_x, col_basis, col_links)
    same_core = [[2 * chip + core for chip in CHIP_ORDER] for core in range(2)]
    same_chip = [[2 * chip, 2 * chip + 1] for chip in range(16)]
    arrived = lax.all_to_all(message, "row", 0, 0, axis_index_groups=same_core)
    blocks, up, down, rows, cols, nearby = call_prepare(
        coupling, col_top_links, row_links, coupling_rows, coupling_cols,
        near_blocks, columns_x, near_rows, near_cols,
    )
    arrived, nearby = lax.optimization_barrier((arrived, nearby))
    gathered = lax.all_gather(arrived, "row", axis=0, axis_index_groups=same_chip)
    partials = call_trees(rows, cols, gathered, up, blocks, down)
    scattered = lax.all_to_all(partials, "col", 0, 0, axis_index_groups=[COL_ORDER])
    return pl.pallas_call(
        output_kernel,
        out_shape=jax.ShapeDtypeStruct((32, 512), BF16),
        in_specs=[vmem()] * 3,
        out_specs=vmem(),
        compiler_params=pltpu.CompilerParams(vmem_limit_bytes=8 * 1024 * 1024),
        name="outputs",
    )(scattered, row_basis, nearby)


def solution(mesh):
    in_specs = (
        P(None, ("row", "col")),
        P(("row", "col"), None, None),
        P(("row", "col"), None),
        P("col", None, None),
        P(("row", "col"), None, None),
        P("row", None, None),
        P(("row", "col"), None),
        P(("row", "col"), None),
        P(("row", "col"), None),
        P(("row", "col"), None, None),
        P(("row", "col")),
        P(("row", "col")),
    )
    out_specs = P(None, ("row", "col"))
    return jax.shard_map(local, mesh=mesh, in_specs=in_specs, out_specs=out_specs, check_vma=False)
```

```python
import jax
import jax.numpy as jnp
from jax import lax
from jax.experimental import pallas as pl
from jax.experimental.pallas import tpu as pltpu
from jax.sharding import PartitionSpec as P

CHIP_ORDER = [(10 + j) % 16 for j in range(16)]

F32 = jnp.float32
BF16 = jnp.bfloat16


def col_start(row):
    return 11 - 3 * ((row % 2) ^ (row < 2))


def dot(a, b):
    return jnp.dot(a, b, preferred_element_type=F32)


def vmem():
    return pl.BlockSpec(memory_space=pltpu.VMEM)


def smem():
    return pl.BlockSpec(memory_space=pltpu.SMEM)


def moments_kernel(x_ref, basis_ref, links_ref, out_ref):
    links = links_ref[...].reshape(2, 64, 64)
    leaves = []
    for i in range(2):
        moment = lax.dot_general(
            x_ref[:, 256 * i : 256 * (i + 1)],
            basis_ref[i],
            (((1,), (1,)), ((), ())),
            preferred_element_type=F32,
        )
        leaves.append(moment.astype(BF16))
    parent = dot(leaves[0], links[0]) + dot(leaves[1], links[1])
    low = jnp.concatenate(leaves, axis=1)
    high = jnp.concatenate([parent[:16], parent[16:]], axis=1).astype(BF16)
    for r in range(out_ref.shape[0]):
        out_ref[r, 0:32, :] = low
        out_ref[r, 32:48, :] = high


def paired(first, second):
    columns = []
    for i in range(0, first.shape[1], 128):
        one, two = first[:, i : i + 128], second[:, i : i + 128]
        columns.append(jnp.concatenate([one[:, 0:64], two[:, 0:64]], axis=1))
        columns.append(jnp.concatenate([one[:, 64:128], two[:, 64:128]], axis=1))
    return jnp.concatenate(columns, axis=1).reshape(first.shape[0], 64, 128)


def prepare_kernel(
    coupling_in, top_in, links_in, rows_in, cols_in, near_in, x_in, near_rows_in, near_cols_in,
    blocks_ref, up_ref, down_ref, rows_ref, cols_ref, nearby_ref,
    coupling_ref, top_ref, links_ref, near_ref, x_ref, near_rows_ref, near_cols_ref, sems,
):
    pairs = (
        (links_in.at[0], links_ref),
        (top_in.at[0], top_ref),
        (coupling_in, coupling_ref),
        (near_rows_in, near_rows_ref),
        (near_cols_in, near_cols_ref),
        (x_in, x_ref),
        (near_in, near_ref),
        (rows_in, rows_ref),
        (cols_in, cols_ref),
    )
    copies = [pltpu.make_async_copy(source, target, sems.at[i]) for i, (source, target) in enumerate(pairs)]
    for copy in copies:
        copy.start()
    copies[0].wait()
    links = links_ref[...].reshape(56, 64, 64)
    for b in range(16):
        one = jnp.concatenate([links[2 * b], links[2 * b + 1]], axis=1)
        two = dot(links[32 + b], one).astype(BF16)
        three = dot(links[48 + b // 2], two).astype(BF16)
        down_ref[b, 0:64, :] = two
        down_ref[b, 64:128, :] = one
        down_ref[b, 128:192, :] = jnp.zeros_like(one)
        down_ref[b, 192:256, :] = three
    copies[1].wait()
    top = top_ref[...].reshape(48, 64, 64)
    for p in range(24):
        up_ref[p] = jnp.concatenate([top[2 * p], top[2 * p + 1]], axis=1)
    copies[2].wait()
    for place, i in ((0, 0), (16, 16), (32, 64), (48, 80)):
        blocks_ref[place : place + 16] = paired(coupling_ref[i : i + 16], coupling_ref[i + 32 : i + 48])
    for copy in copies[3:7]:
        copy.wait()
    nearby_ref[...] = jnp.zeros_like(nearby_ref)
    for s in range(8):
        start = pl.multiple_of(near_cols_ref[s] * 256, 256)
        nearby_ref[near_rows_ref[s]] += dot(x_ref[:, pl.ds(start, 256)], near_ref[s])
    for copy in copies[7:]:
        copy.wait()


def tree_kernel(
    rows_ref, cols_ref, got_ref, top_ref, coupling_ref, down_ref, out_ref,
    mom0, mom1, mom2, mom3, acc0, acc1, acc2, acc3,
):
    mom, acc = (mom0, mom1, mom2, mom3), (acc0, acc1, acc2, acc3)
    for depth in range(4):
        acc[depth][...] = jnp.zeros_like(acc[depth])
    received = [(2 * chip + core, core, j) for j, chip in enumerate(CHIP_ORDER) for core in range(2)]
    for a, core, j in received:
        parent = got_ref[core, j, 32:48, :]
        mom1[a, 0:16] = parent[:, 0:64]
        mom1[a, 16:32] = parent[:, 64:128]
    for p in range(16):
        both = dot(mom1[2 * p : 2 * p + 2].reshape(64, 64), top_ref[p])
        mom2[p] = (both[0:32, 0:64] + both[32:64, 64:128]).astype(BF16)
    for a, core, j in received:
        both = got_ref[core, j, 0:32, :]
        mom0[2 * a] = both[:, 0:64]
        mom0[2 * a + 1] = both[:, 64:128]
    for p in range(8):
        both = dot(mom2[2 * p : 2 * p + 2].reshape(64, 64), top_ref[16 + p])
        mom3[p] = (both[0:32, 0:64] + both[32:64, 64:128]).astype(BF16)
    for depth in (0, 2):
        for s in range(32):
            first, second = cols_ref[depth, s], cols_ref[depth + 1, s]
            picked = jnp.concatenate([mom[depth][first], mom[depth + 1][second]], axis=0)
            term = dot(picked, coupling_ref[depth * 16 + s])
            acc[depth][rows_ref[depth, s], :, 0:64] += term[0:32, 0:64]
            acc[depth + 1][rows_ref[depth + 1, s], :, 64:128] += term[32:64, 64:128]
    tops = [acc3[p].astype(BF16) for p in range(4)]
    start = col_start(lax.axis_index("row"))
    for b in range(16):
        upper = jnp.concatenate([(acc1[b] + acc2[b // 2]).astype(BF16), tops[b // 4]], axis=1)
        own = jnp.concatenate([acc0[2 * b], acc0[2 * b + 1]], axis=1)
        out_ref[lax.rem(16 + b - start, 16)] = (own + dot(upper, down_ref[b])).astype(BF16)


def output_kernel(got_ref, basis_ref, near_ref, out_ref):
    total = got_ref[0].astype(F32)
    for b in range(1, got_ref.shape[0]):
        total += got_ref[b].astype(F32)
    leaf_local = total.astype(BF16)
    for i in range(2):
        distant = dot(leaf_local[:, 64 * i : 64 * (i + 1)], basis_ref[i])
        out_ref[:, 256 * i : 256 * (i + 1)] = (distant + near_ref[i]).astype(BF16)


def call_prepare(*operands):
    return pl.pallas_call(
        prepare_kernel,
        out_shape=[
            pltpu.VMEM((64, 64, 128), BF16),
            pltpu.VMEM((24, 64, 128), BF16),
            pltpu.VMEM((16, 256, 128), BF16),
            pltpu.SMEM((4, 32), jnp.int32),
            pltpu.SMEM((4, 32), jnp.int32),
            pltpu.VMEM((2, 32, 256), F32),
        ],
        in_specs=[pl.BlockSpec(memory_space=pl.ANY)] * 9,
        out_specs=[vmem()] * 3 + [smem()] * 2 + [vmem()],
        scratch_shapes=[
            pltpu.VMEM((128, 4096), BF16),
            pltpu.VMEM((48, 4096), BF16),
            pltpu.VMEM((56, 4096), BF16),
            pltpu.VMEM((8, 256, 256), BF16),
            pltpu.VMEM((32, 512), BF16),
            pltpu.SMEM((8,), jnp.int32),
            pltpu.SMEM((8,), jnp.int32),
            pltpu.SemaphoreType.DMA((9,)),
        ],
        compiler_params=pltpu.CompilerParams(vmem_limit_bytes=60 * 1024 * 1024),
        cost_estimate=pl.CostEstimate(flops=33_554_432, bytes_accessed=8_000_000, transcendentals=0),
        name="prepare",
    )(*operands)


def call_trees(*operands):
    return pl.pallas_call(
        tree_kernel,
        out_shape=jax.ShapeDtypeStruct((16, 32, 128), BF16),
        in_specs=[smem()] * 2 + [vmem()] * 4,
        out_specs=vmem(),
        scratch_shapes=[pltpu.VMEM((64 >> depth, 32, 64), BF16) for depth in range(4)]
        + [pltpu.VMEM((32 >> depth, 32, 128 if depth else 64), F32) for depth in range(4)],
        compiler_params=pltpu.CompilerParams(vmem_limit_bytes=16 * 1024 * 1024),
        name="trees",
    )(*operands)


def local(
    columns_x,
    col_basis,
    col_links,
    col_top_links,
    row_basis,
    row_links,
    coupling,
    coupling_rows,
    coupling_cols,
    near_blocks,
    near_rows,
    near_cols,
):
    message = pl.pallas_call(
        moments_kernel,
        out_shape=jax.ShapeDtypeStruct((16, 48, 128), BF16),
        in_specs=[vmem()] * 3,
        out_specs=vmem(),
        name="moments",
    )(columns_x, col_basis, col_links)
    same_core = [[2 * chip + core for chip in CHIP_ORDER] for core in range(2)]
    same_chip = [[2 * chip, 2 * chip + 1] for chip in range(16)]
    arrived = lax.all_to_all(message, "row", 0, 0, axis_index_groups=same_core)
    blocks, up, down, rows, cols, nearby = call_prepare(
        coupling, col_top_links, row_links, coupling_rows, coupling_cols,
        near_blocks, columns_x, near_rows, near_cols,
    )
    arrived, nearby = lax.optimization_barrier((arrived, nearby))
    gathered = lax.all_gather(arrived, "row", axis=0, axis_index_groups=same_chip)
    partials = call_trees(rows, cols, gathered, up, blocks, down)
    same_row = [[16 * row + (col_start(row) + j) % 16 for j in range(16)] for row in range(32)]
    scattered = lax.all_to_all(partials, ("row", "col"), 0, 0, axis_index_groups=same_row)
    return pl.pallas_call(
        output_kernel,
        out_shape=jax.ShapeDtypeStruct((32, 512), BF16),
        in_specs=[vmem()] * 3,
        out_specs=vmem(),
        compiler_params=pltpu.CompilerParams(vmem_limit_bytes=8 * 1024 * 1024),
        name="outputs",
    )(scattered, row_basis, nearby)


def solution(mesh):
    in_specs = (
        P(None, ("row", "col")),
        P(("row", "col"), None, None),
        P(("row", "col"), None),
        P("col", None, None),
        P(("row", "col"), None, None),
        P("row", None, None),
        P(("row", "col"), None),
        P(("row", "col"), None),
        P(("row", "col"), None),
        P(("row", "col"), None, None),
        P(("row", "col")),
        P(("row", "col")),
    )
    out_specs = P(None, ("row", "col"))
    return jax.shard_map(local, mesh=mesh, in_specs=in_specs, out_specs=out_specs, check_vma=False)
```

```python
import jax
import jax.numpy as jnp
from jax import lax
from jax.experimental import pallas as pl
from jax.experimental.pallas import tpu as pltpu
from jax.sharding import PartitionSpec as P

CHIP_ORDER = [(10 + j) % 16 for j in range(16)]

F32 = jnp.float32
BF16 = jnp.bfloat16


def col_start(row):
    return 11 - 3 * (row % 2)


def dot(a, b):
    return jnp.dot(a, b, preferred_element_type=F32)


def vmem():
    return pl.BlockSpec(memory_space=pltpu.VMEM)


def smem():
    return pl.BlockSpec(memory_space=pltpu.SMEM)


def moments_kernel(x_ref, basis_ref, links_ref, out_ref):
    links = links_ref[...].reshape(2, 64, 64)
    leaves = []
    for i in range(2):
        moment = lax.dot_general(
            x_ref[:, 256 * i : 256 * (i + 1)],
            basis_ref[i],
            (((1,), (1,)), ((), ())),
            preferred_element_type=F32,
        )
        leaves.append(moment.astype(BF16))
    parent = dot(leaves[0], links[0]) + dot(leaves[1], links[1])
    low = jnp.concatenate(leaves, axis=1)
    high = jnp.concatenate([parent[:16], parent[16:]], axis=1).astype(BF16)
    for r in range(out_ref.shape[0]):
        out_ref[r, 0:32, :] = low
        out_ref[r, 32:48, :] = high


def paired(first, second):
    columns = []
    for i in range(0, first.shape[1], 128):
        one, two = first[:, i : i + 128], second[:, i : i + 128]
        columns.append(jnp.concatenate([one[:, 0:64], two[:, 0:64]], axis=1))
        columns.append(jnp.concatenate([one[:, 64:128], two[:, 64:128]], axis=1))
    return jnp.concatenate(columns, axis=1).reshape(first.shape[0], 64, 128)


def prepare_kernel(
    coupling_in, top_in, links_in, rows_in, cols_in, near_in, x_in, near_rows_in, near_cols_in,
    blocks_ref, up_ref, down_ref, rows_ref, cols_ref, nearby_ref,
    coupling_ref, top_ref, links_ref, near_ref, x_ref, near_rows_ref, near_cols_ref, sems,
):
    pairs = (
        (links_in.at[0], links_ref),
        (top_in.at[0], top_ref),
        (coupling_in, coupling_ref),
        (near_rows_in, near_rows_ref),
        (near_cols_in, near_cols_ref),
        (x_in, x_ref),
        (near_in, near_ref),
        (rows_in, rows_ref),
        (cols_in, cols_ref),
    )
    copies = [pltpu.make_async_copy(source, target, sems.at[i]) for i, (source, target) in enumerate(pairs)]
    for copy in copies:
        copy.start()
    copies[0].wait()
    links = links_ref[...].reshape(56, 64, 64)
    for b in range(16):
        one = jnp.concatenate([links[2 * b], links[2 * b + 1]], axis=1)
        two = dot(links[32 + b], one).astype(BF16)
        three = dot(links[48 + b // 2], two).astype(BF16)
        down_ref[b, 0:64, :] = two
        down_ref[b, 64:128, :] = one
        down_ref[b, 128:192, :] = jnp.zeros_like(one)
        down_ref[b, 192:256, :] = three
    copies[1].wait()
    top = top_ref[...].reshape(48, 64, 64)
    for p in range(24):
        up_ref[p] = jnp.concatenate([top[2 * p], top[2 * p + 1]], axis=1)
    copies[2].wait()
    for place, i in ((0, 0), (16, 16), (32, 64), (48, 80)):
        blocks_ref[place : place + 16] = paired(coupling_ref[i : i + 16], coupling_ref[i + 32 : i + 48])
    for copy in copies[3:7]:
        copy.wait()
    nearby_ref[...] = jnp.zeros_like(nearby_ref)
    for s in range(8):
        start = pl.multiple_of(near_cols_ref[s] * 256, 256)
        nearby_ref[near_rows_ref[s]] += dot(x_ref[:, pl.ds(start, 256)], near_ref[s])
    for copy in copies[7:]:
        copy.wait()


def tree_kernel(
    rows_ref, cols_ref, got_ref, top_ref, coupling_ref, down_ref, out_ref,
    mom0, mom1, mom2, mom3, acc0, acc1, acc2, acc3,
):
    mom, acc = (mom0, mom1, mom2, mom3), (acc0, acc1, acc2, acc3)
    for depth in range(4):
        acc[depth][...] = jnp.zeros_like(acc[depth])
    received = [(2 * chip + core, core, j) for j, chip in enumerate(CHIP_ORDER) for core in range(2)]
    for a, core, j in received:
        parent = got_ref[core, j, 32:48, :]
        mom1[a, 0:16] = parent[:, 0:64]
        mom1[a, 16:32] = parent[:, 64:128]
    for p in range(16):
        both = dot(mom1[2 * p : 2 * p + 2].reshape(64, 64), top_ref[p])
        mom2[p] = (both[0:32, 0:64] + both[32:64, 64:128]).astype(BF16)
    for a, core, j in received:
        both = got_ref[core, j, 0:32, :]
        mom0[2 * a] = both[:, 0:64]
        mom0[2 * a + 1] = both[:, 64:128]
    for p in range(8):
        both = dot(mom2[2 * p : 2 * p + 2].reshape(64, 64), top_ref[16 + p])
        mom3[p] = (both[0:32, 0:64] + both[32:64, 64:128]).astype(BF16)
    for depth in (0, 2):
        for s in range(32):
            first, second = cols_ref[depth, s], cols_ref[depth + 1, s]
            picked = jnp.concatenate([mom[depth][first], mom[depth + 1][second]], axis=0)
            term = dot(picked, coupling_ref[depth * 16 + s])
            acc[depth][rows_ref[depth, s], :, 0:64] += term[0:32, 0:64]
            acc[depth + 1][rows_ref[depth + 1, s], :, 64:128] += term[32:64, 64:128]
    tops = [acc3[p].astype(BF16) for p in range(4)]
    start = col_start(lax.axis_index("row"))
    for b in range(16):
        upper = jnp.concatenate([(acc1[b] + acc2[b // 2]).astype(BF16), tops[b // 4]], axis=1)
        own = jnp.concatenate([acc0[2 * b], acc0[2 * b + 1]], axis=1)
        out_ref[lax.rem(16 + b - start, 16)] = (own + dot(upper, down_ref[b])).astype(BF16)


def output_kernel(got_ref, basis_ref, near_ref, out_ref):
    total = got_ref[0].astype(F32)
    for b in range(1, got_ref.shape[0]):
        total += got_ref[b].astype(F32)
    leaf_local = total.astype(BF16)
    for i in range(2):
        distant = dot(leaf_local[:, 64 * i : 64 * (i + 1)], basis_ref[i])
        out_ref[:, 256 * i : 256 * (i + 1)] = (distant + near_ref[i]).astype(BF16)


def call_prepare(*operands):
    return pl.pallas_call(
        prepare_kernel,
        out_shape=[
            pltpu.VMEM((64, 64, 128), BF16),
            pltpu.VMEM((24, 64, 128), BF16),
            pltpu.VMEM((16, 256, 128), BF16),
            pltpu.SMEM((4, 32), jnp.int32),
            pltpu.SMEM((4, 32), jnp.int32),
            pltpu.VMEM((2, 32, 256), F32),
        ],
        in_specs=[pl.BlockSpec(memory_space=pl.ANY)] * 9,
        out_specs=[vmem()] * 3 + [smem()] * 2 + [vmem()],
        scratch_shapes=[
            pltpu.VMEM((128, 4096), BF16),
            pltpu.VMEM((48, 4096), BF16),
            pltpu.VMEM((56, 4096), BF16),
            pltpu.VMEM((8, 256, 256), BF16),
            pltpu.VMEM((32, 512), BF16),
            pltpu.SMEM((8,), jnp.int32),
            pltpu.SMEM((8,), jnp.int32),
            pltpu.SemaphoreType.DMA((9,)),
        ],
        compiler_params=pltpu.CompilerParams(vmem_limit_bytes=60 * 1024 * 1024),
        cost_estimate=pl.CostEstimate(flops=33_554_432, bytes_accessed=8_000_000, transcendentals=0),
        name="prepare",
    )(*operands)


def call_trees(*operands):
    return pl.pallas_call(
        tree_kernel,
        out_shape=jax.ShapeDtypeStruct((16, 32, 128), BF16),
        in_specs=[smem()] * 2 + [vmem()] * 4,
        out_specs=vmem(),
        scratch_shapes=[pltpu.VMEM((64 >> depth, 32, 64), BF16) for depth in range(4)]
        + [pltpu.VMEM((32 >> depth, 32, 128 if depth else 64), F32) for depth in range(4)],
        compiler_params=pltpu.CompilerParams(vmem_limit_bytes=16 * 1024 * 1024),
        name="trees",
    )(*operands)


def local(
    columns_x,
    col_basis,
    col_links,
    col_top_links,
    row_basis,
    row_links,
    coupling,
    coupling_rows,
    coupling_cols,
    near_blocks,
    near_rows,
    near_cols,
):
    message = pl.pallas_call(
        moments_kernel,
        out_shape=jax.ShapeDtypeStruct((16, 48, 128), BF16),
        in_specs=[vmem()] * 3,
        out_specs=vmem(),
        name="moments",
    )(columns_x, col_basis, col_links)
    same_core = [[2 * chip + core for chip in CHIP_ORDER] for core in range(2)]
    same_chip = [[2 * chip, 2 * chip + 1] for chip in range(16)]
    arrived = lax.all_to_all(message, "row", 0, 0, axis_index_groups=same_core)
    blocks, up, down, rows, cols, nearby = call_prepare(
        coupling, col_top_links, row_links, coupling_rows, coupling_cols,
        near_blocks, columns_x, near_rows, near_cols,
    )
    arrived, nearby = lax.optimization_barrier((arrived, nearby))
    gathered = lax.all_gather(arrived, "row", axis=0, axis_index_groups=same_chip)
    partials = call_trees(rows, cols, gathered, up, blocks, down)
    same_row = [[16 * row + (col_start(row) + j) % 16 for j in range(16)] for row in range(32)]
    scattered = lax.all_to_all(partials, ("row", "col"), 0, 0, axis_index_groups=same_row)
    return pl.pallas_call(
        output_kernel,
        out_shape=jax.ShapeDtypeStruct((32, 512), BF16),
        in_specs=[vmem()] * 3,
        out_specs=vmem(),
        compiler_params=pltpu.CompilerParams(vmem_limit_bytes=8 * 1024 * 1024),
        name="outputs",
    )(scattered, row_basis, nearby)


def solution(mesh):
    in_specs = (
        P(None, ("row", "col")),
        P(("row", "col"), None, None),
        P(("row", "col"), None),
        P("col", None, None),
        P(("row", "col"), None, None),
        P("row", None, None),
        P(("row", "col"), None),
        P(("row", "col"), None),
        P(("row", "col"), None),
        P(("row", "col"), None, None),
        P(("row", "col")),
        P(("row", "col")),
    )
    out_specs = P(None, ("row", "col"))
    return jax.shard_map(local, mesh=mesh, in_specs=in_specs, out_specs=out_specs, check_vma=False)
```

```python
import jax
import jax.numpy as jnp
from jax import lax
from jax.experimental import pallas as pl
from jax.experimental.pallas import tpu as pltpu
from jax.sharding import PartitionSpec as P

CHIP_ORDER = [(10 + j) % 16 for j in range(16)]

F32 = jnp.float32
BF16 = jnp.bfloat16


def col_start(row):
    return 10 - 2 * (row % 2)


def dot(a, b):
    return jnp.dot(a, b, preferred_element_type=F32)


def vmem():
    return pl.BlockSpec(memory_space=pltpu.VMEM)


def smem():
    return pl.BlockSpec(memory_space=pltpu.SMEM)


def moments_kernel(x_ref, basis_ref, links_ref, out_ref):
    links = links_ref[...].reshape(2, 64, 64)
    leaves = []
    for i in range(2):
        moment = lax.dot_general(
            x_ref[:, 256 * i : 256 * (i + 1)],
            basis_ref[i],
            (((1,), (1,)), ((), ())),
            preferred_element_type=F32,
        )
        leaves.append(moment.astype(BF16))
    parent = dot(leaves[0], links[0]) + dot(leaves[1], links[1])
    low = jnp.concatenate(leaves, axis=1)
    high = jnp.concatenate([parent[:16], parent[16:]], axis=1).astype(BF16)
    for r in range(out_ref.shape[0]):
        out_ref[r, 0:32, :] = low
        out_ref[r, 32:48, :] = high


def paired(first, second):
    columns = []
    for i in range(0, first.shape[1], 128):
        one, two = first[:, i : i + 128], second[:, i : i + 128]
        columns.append(jnp.concatenate([one[:, 0:64], two[:, 0:64]], axis=1))
        columns.append(jnp.concatenate([one[:, 64:128], two[:, 64:128]], axis=1))
    return jnp.concatenate(columns, axis=1).reshape(first.shape[0], 64, 128)


def prepare_kernel(
    coupling_in, top_in, links_in, rows_in, cols_in, near_in, x_in, near_rows_in, near_cols_in,
    blocks_ref, up_ref, down_ref, rows_ref, cols_ref, nearby_ref,
    coupling_ref, top_ref, links_ref, near_ref, x_ref, near_rows_ref, near_cols_ref, sems,
):
    pairs = (
        (links_in.at[0], links_ref),
        (top_in.at[0], top_ref),
        (coupling_in, coupling_ref),
        (near_rows_in, near_rows_ref),
        (near_cols_in, near_cols_ref),
        (x_in, x_ref),
        (near_in, near_ref),
        (rows_in, rows_ref),
        (cols_in, cols_ref),
    )
    copies = [pltpu.make_async_copy(source, target, sems.at[i]) for i, (source, target) in enumerate(pairs)]
    for copy in copies:
        copy.start()
    copies[0].wait()
    links = links_ref[...].reshape(56, 64, 64)
    for b in range(16):
        one = jnp.concatenate([links[2 * b], links[2 * b + 1]], axis=1)
        two = dot(links[32 + b], one).astype(BF16)
        three = dot(links[48 + b // 2], two).astype(BF16)
        down_ref[b, 0:64, :] = two
        down_ref[b, 64:128, :] = one
        down_ref[b, 128:192, :] = jnp.zeros_like(one)
        down_ref[b, 192:256, :] = three
    copies[1].wait()
    top = top_ref[...].reshape(48, 64, 64)
    for p in range(24):
        up_ref[p] = jnp.concatenate([top[2 * p], top[2 * p + 1]], axis=1)
    copies[2].wait()
    for place, i in ((0, 0), (16, 16), (32, 64), (48, 80)):
        blocks_ref[place : place + 16] = paired(coupling_ref[i : i + 16], coupling_ref[i + 32 : i + 48])
    for copy in copies[3:7]:
        copy.wait()
    nearby_ref[...] = jnp.zeros_like(nearby_ref)
    for s in range(8):
        start = pl.multiple_of(near_cols_ref[s] * 256, 256)
        nearby_ref[near_rows_ref[s]] += dot(x_ref[:, pl.ds(start, 256)], near_ref[s])
    for copy in copies[7:]:
        copy.wait()


def tree_kernel(
    rows_ref, cols_ref, got_ref, top_ref, coupling_ref, down_ref, out_ref,
    mom0, mom1, mom2, mom3, acc0, acc1, acc2, acc3,
):
    mom, acc = (mom0, mom1, mom2, mom3), (acc0, acc1, acc2, acc3)
    for depth in range(4):
        acc[depth][...] = jnp.zeros_like(acc[depth])
    received = [(2 * chip + core, core, j) for j, chip in enumerate(CHIP_ORDER) for core in range(2)]
    for a, core, j in received:
        parent = got_ref[core, j, 32:48, :]
        mom1[a, 0:16] = parent[:, 0:64]
        mom1[a, 16:32] = parent[:, 64:128]
    for p in range(16):
        both = dot(mom1[2 * p : 2 * p + 2].reshape(64, 64), top_ref[p])
        mom2[p] = (both[0:32, 0:64] + both[32:64, 64:128]).astype(BF16)
    for a, core, j in received:
        both = got_ref[core, j, 0:32, :]
        mom0[2 * a] = both[:, 0:64]
        mom0[2 * a + 1] = both[:, 64:128]
    for p in range(8):
        both = dot(mom2[2 * p : 2 * p + 2].reshape(64, 64), top_ref[16 + p])
        mom3[p] = (both[0:32, 0:64] + both[32:64, 64:128]).astype(BF16)
    for depth in (0, 2):
        for s in range(32):
            first, second = cols_ref[depth, s], cols_ref[depth + 1, s]
            picked = jnp.concatenate([mom[depth][first], mom[depth + 1][second]], axis=0)
            term = dot(picked, coupling_ref[depth * 16 + s])
            acc[depth][rows_ref[depth, s], :, 0:64] += term[0:32, 0:64]
            acc[depth + 1][rows_ref[depth + 1, s], :, 64:128] += term[32:64, 64:128]
    tops = [acc3[p].astype(BF16) for p in range(4)]
    start = col_start(lax.axis_index("row"))
    for b in range(16):
        upper = jnp.concatenate([(acc1[b] + acc2[b // 2]).astype(BF16), tops[b // 4]], axis=1)
        own = jnp.concatenate([acc0[2 * b], acc0[2 * b + 1]], axis=1)
        out_ref[lax.rem(16 + b - start, 16)] = (own + dot(upper, down_ref[b])).astype(BF16)


def output_kernel(got_ref, basis_ref, near_ref, out_ref):
    total = got_ref[0].astype(F32)
    for b in range(1, got_ref.shape[0]):
        total += got_ref[b].astype(F32)
    leaf_local = total.astype(BF16)
    for i in range(2):
        distant = dot(leaf_local[:, 64 * i : 64 * (i + 1)], basis_ref[i])
        out_ref[:, 256 * i : 256 * (i + 1)] = (distant + near_ref[i]).astype(BF16)


def call_prepare(*operands):
    return pl.pallas_call(
        prepare_kernel,
        out_shape=[
            pltpu.VMEM((64, 64, 128), BF16),
            pltpu.VMEM((24, 64, 128), BF16),
            pltpu.VMEM((16, 256, 128), BF16),
            pltpu.SMEM((4, 32), jnp.int32),
            pltpu.SMEM((4, 32), jnp.int32),
            pltpu.VMEM((2, 32, 256), F32),
        ],
        in_specs=[pl.BlockSpec(memory_space=pl.ANY)] * 9,
        out_specs=[vmem()] * 3 + [smem()] * 2 + [vmem()],
        scratch_shapes=[
            pltpu.VMEM((128, 4096), BF16),
            pltpu.VMEM((48, 4096), BF16),
            pltpu.VMEM((56, 4096), BF16),
            pltpu.VMEM((8, 256, 256), BF16),
            pltpu.VMEM((32, 512), BF16),
            pltpu.SMEM((8,), jnp.int32),
            pltpu.SMEM((8,), jnp.int32),
            pltpu.SemaphoreType.DMA((9,)),
        ],
        compiler_params=pltpu.CompilerParams(vmem_limit_bytes=60 * 1024 * 1024),
        cost_estimate=pl.CostEstimate(flops=33_554_432, bytes_accessed=8_000_000, transcendentals=0),
        name="prepare",
    )(*operands)


def call_trees(*operands):
    return pl.pallas_call(
        tree_kernel,
        out_shape=jax.ShapeDtypeStruct((16, 32, 128), BF16),
        in_specs=[smem()] * 2 + [vmem()] * 4,
        out_specs=vmem(),
        scratch_shapes=[pltpu.VMEM((64 >> depth, 32, 64), BF16) for depth in range(4)]
        + [pltpu.VMEM((32 >> depth, 32, 128 if depth else 64), F32) for depth in range(4)],
        compiler_params=pltpu.CompilerParams(vmem_limit_bytes=16 * 1024 * 1024),
        name="trees",
    )(*operands)


def local(
    columns_x,
    col_basis,
    col_links,
    col_top_links,
    row_basis,
    row_links,
    coupling,
    coupling_rows,
    coupling_cols,
    near_blocks,
    near_rows,
    near_cols,
):
    message = pl.pallas_call(
        moments_kernel,
        out_shape=jax.ShapeDtypeStruct((16, 48, 128), BF16),
        in_specs=[vmem()] * 3,
        out_specs=vmem(),
        name="moments",
    )(columns_x, col_basis, col_links)
    same_core = [[2 * chip + core for chip in CHIP_ORDER] for core in range(2)]
    same_chip = [[2 * chip, 2 * chip + 1] for chip in range(16)]
    arrived = lax.all_to_all(message, "row", 0, 0, axis_index_groups=same_core)
    blocks, up, down, rows, cols, nearby = call_prepare(
        coupling, col_top_links, row_links, coupling_rows, coupling_cols,
        near_blocks, columns_x, near_rows, near_cols,
    )
    arrived, nearby = lax.optimization_barrier((arrived, nearby))
    gathered = lax.all_gather(arrived, "row", axis=0, axis_index_groups=same_chip)
    partials = call_trees(rows, cols, gathered, up, blocks, down)
    same_row = [[16 * row + (col_start(row) + j) % 16 for j in range(16)] for row in range(32)]
    scattered = lax.all_to_all(partials, ("row", "col"), 0, 0, axis_index_groups=same_row)
    return pl.pallas_call(
        output_kernel,
        out_shape=jax.ShapeDtypeStruct((32, 512), BF16),
        in_specs=[vmem()] * 3,
        out_specs=vmem(),
        compiler_params=pltpu.CompilerParams(vmem_limit_bytes=8 * 1024 * 1024),
        name="outputs",
    )(scattered, row_basis, nearby)


def solution(mesh):
    in_specs = (
        P(None, ("row", "col")),
        P(("row", "col"), None, None),
        P(("row", "col"), None),
        P("col", None, None),
        P(("row", "col"), None, None),
        P("row", None, None),
        P(("row", "col"), None),
        P(("row", "col"), None),
        P(("row", "col"), None),
        P(("row", "col"), None, None),
        P(("row", "col")),
        P(("row", "col")),
    )
    out_specs = P(None, ("row", "col"))
    return jax.shard_map(local, mesh=mesh, in_specs=in_specs, out_specs=out_specs, check_vma=False)
```

```python
import jax
import jax.numpy as jnp
from jax import lax
from jax.experimental import pallas as pl
from jax.experimental.pallas import tpu as pltpu
from jax.sharding import PartitionSpec as P

CHIP_ORDER = [(10 + j) % 16 for j in range(16)]
COL_ORDERS = (
    [11, 1, 0, 3, 2, 5, 4, 7, 6, 15, 14, 13, 12, 10, 9, 8],
    [8, 0, 1, 2, 3, 4, 5, 6, 7, 15, 14, 13, 12, 11, 10, 9],
)

F32 = jnp.float32
BF16 = jnp.bfloat16


def dot(a, b):
    return jnp.dot(a, b, preferred_element_type=F32)


def vmem():
    return pl.BlockSpec(memory_space=pltpu.VMEM)


def smem():
    return pl.BlockSpec(memory_space=pltpu.SMEM)


def moments_kernel(x_ref, basis_ref, links_ref, out_ref):
    links = links_ref[...].reshape(2, 64, 64)
    leaves = []
    for i in range(2):
        moment = lax.dot_general(
            x_ref[:, 256 * i : 256 * (i + 1)],
            basis_ref[i],
            (((1,), (1,)), ((), ())),
            preferred_element_type=F32,
        )
        leaves.append(moment.astype(BF16))
    parent = dot(leaves[0], links[0]) + dot(leaves[1], links[1])
    low = jnp.concatenate(leaves, axis=1)
    high = jnp.concatenate([parent[:16], parent[16:]], axis=1).astype(BF16)
    for r in range(out_ref.shape[0]):
        out_ref[r, 0:32, :] = low
        out_ref[r, 32:48, :] = high


def paired(first, second):
    columns = []
    for i in range(0, first.shape[1], 128):
        one, two = first[:, i : i + 128], second[:, i : i + 128]
        columns.append(jnp.concatenate([one[:, 0:64], two[:, 0:64]], axis=1))
        columns.append(jnp.concatenate([one[:, 64:128], two[:, 64:128]], axis=1))
    return jnp.concatenate(columns, axis=1).reshape(first.shape[0], 64, 128)


def prepare_kernel(
    coupling_in, top_in, links_in, rows_in, cols_in, near_in, x_in, near_rows_in, near_cols_in,
    blocks_ref, up_ref, down_ref, rows_ref, cols_ref, nearby_ref,
    coupling_ref, top_ref, links_ref, near_ref, x_ref, near_rows_ref, near_cols_ref, sems,
):
    pairs = (
        (links_in.at[0], links_ref),
        (top_in.at[0], top_ref),
        (coupling_in, coupling_ref),
        (near_rows_in, near_rows_ref),
        (near_cols_in, near_cols_ref),
        (x_in, x_ref),
        (near_in, near_ref),
        (rows_in, rows_ref),
        (cols_in, cols_ref),
    )
    copies = [pltpu.make_async_copy(source, target, sems.at[i]) for i, (source, target) in enumerate(pairs)]
    for copy in copies:
        copy.start()
    copies[0].wait()
    links = links_ref[...].reshape(56, 64, 64)
    for b in range(16):
        one = jnp.concatenate([links[2 * b], links[2 * b + 1]], axis=1)
        two = dot(links[32 + b], one).astype(BF16)
        three = dot(links[48 + b // 2], two).astype(BF16)
        down_ref[b, 0:64, :] = two
        down_ref[b, 64:128, :] = one
        down_ref[b, 128:192, :] = jnp.zeros_like(one)
        down_ref[b, 192:256, :] = three
    copies[1].wait()
    top = top_ref[...].reshape(48, 64, 64)
    for p in range(24):
        up_ref[p] = jnp.concatenate([top[2 * p], top[2 * p + 1]], axis=1)
    copies[2].wait()
    for place, i in ((0, 0), (16, 16), (32, 64), (48, 80)):
        blocks_ref[place : place + 16] = paired(coupling_ref[i : i + 16], coupling_ref[i + 32 : i + 48])
    for copy in copies[3:7]:
        copy.wait()
    nearby_ref[...] = jnp.zeros_like(nearby_ref)
    for s in range(8):
        start = pl.multiple_of(near_cols_ref[s] * 256, 256)
        nearby_ref[near_rows_ref[s]] += dot(x_ref[:, pl.ds(start, 256)], near_ref[s])
    for copy in copies[7:]:
        copy.wait()


def tree_kernel(
    rows_ref, cols_ref, got_ref, top_ref, coupling_ref, down_ref, out_ref,
    mom0, mom1, mom2, mom3, acc0, acc1, acc2, acc3,
):
    mom, acc = (mom0, mom1, mom2, mom3), (acc0, acc1, acc2, acc3)
    for depth in range(4):
        acc[depth][...] = jnp.zeros_like(acc[depth])
    received = [(2 * chip + core, core, j) for j, chip in enumerate(CHIP_ORDER) for core in range(2)]
    for a, core, j in received:
        parent = got_ref[core, j, 32:48, :]
        mom1[a, 0:16] = parent[:, 0:64]
        mom1[a, 16:32] = parent[:, 64:128]
    for p in range(16):
        both = dot(mom1[2 * p : 2 * p + 2].reshape(64, 64), top_ref[p])
        mom2[p] = (both[0:32, 0:64] + both[32:64, 64:128]).astype(BF16)
    for a, core, j in received:
        both = got_ref[core, j, 0:32, :]
        mom0[2 * a] = both[:, 0:64]
        mom0[2 * a + 1] = both[:, 64:128]
    for p in range(8):
        both = dot(mom2[2 * p : 2 * p + 2].reshape(64, 64), top_ref[16 + p])
        mom3[p] = (both[0:32, 0:64] + both[32:64, 64:128]).astype(BF16)
    for depth in (0, 2):
        for s in range(32):
            first, second = cols_ref[depth, s], cols_ref[depth + 1, s]
            picked = jnp.concatenate([mom[depth][first], mom[depth + 1][second]], axis=0)
            term = dot(picked, coupling_ref[depth * 16 + s])
            acc[depth][rows_ref[depth, s], :, 0:64] += term[0:32, 0:64]
            acc[depth + 1][rows_ref[depth + 1, s], :, 64:128] += term[32:64, 64:128]
    tops = [acc3[p].astype(BF16) for p in range(4)]
    core = lax.rem(lax.axis_index("row"), 2)
    for b in range(16):
        upper = jnp.concatenate([(acc1[b] + acc2[b // 2]).astype(BF16), tops[b // 4]], axis=1)
        own = jnp.concatenate([acc0[2 * b], acc0[2 * b + 1]], axis=1)
        place = jnp.where(core == 0, COL_ORDERS[0].index(b), COL_ORDERS[1].index(b))
        out_ref[place] = (own + dot(upper, down_ref[b])).astype(BF16)


def output_kernel(got_ref, basis_ref, near_ref, out_ref):
    total = got_ref[0].astype(F32)
    for b in range(1, got_ref.shape[0]):
        total += got_ref[b].astype(F32)
    leaf_local = total.astype(BF16)
    for i in range(2):
        distant = dot(leaf_local[:, 64 * i : 64 * (i + 1)], basis_ref[i])
        out_ref[:, 256 * i : 256 * (i + 1)] = (distant + near_ref[i]).astype(BF16)


def call_prepare(*operands):
    return pl.pallas_call(
        prepare_kernel,
        out_shape=[
            pltpu.VMEM((64, 64, 128), BF16),
            pltpu.VMEM((24, 64, 128), BF16),
            pltpu.VMEM((16, 256, 128), BF16),
            pltpu.SMEM((4, 32), jnp.int32),
            pltpu.SMEM((4, 32), jnp.int32),
            pltpu.VMEM((2, 32, 256), F32),
        ],
        in_specs=[pl.BlockSpec(memory_space=pl.ANY)] * 9,
        out_specs=[vmem()] * 3 + [smem()] * 2 + [vmem()],
        scratch_shapes=[
            pltpu.VMEM((128, 4096), BF16),
            pltpu.VMEM((48, 4096), BF16),
            pltpu.VMEM((56, 4096), BF16),
            pltpu.VMEM((8, 256, 256), BF16),
            pltpu.VMEM((32, 512), BF16),
            pltpu.SMEM((8,), jnp.int32),
            pltpu.SMEM((8,), jnp.int32),
            pltpu.SemaphoreType.DMA((9,)),
        ],
        compiler_params=pltpu.CompilerParams(vmem_limit_bytes=60 * 1024 * 1024),
        cost_estimate=pl.CostEstimate(flops=33_554_432, bytes_accessed=8_000_000, transcendentals=0),
        name="prepare",
    )(*operands)


def call_trees(*operands):
    return pl.pallas_call(
        tree_kernel,
        out_shape=jax.ShapeDtypeStruct((16, 32, 128), BF16),
        in_specs=[smem()] * 2 + [vmem()] * 4,
        out_specs=vmem(),
        scratch_shapes=[pltpu.VMEM((64 >> depth, 32, 64), BF16) for depth in range(4)]
        + [pltpu.VMEM((32 >> depth, 32, 128 if depth else 64), F32) for depth in range(4)],
        compiler_params=pltpu.CompilerParams(vmem_limit_bytes=16 * 1024 * 1024),
        name="trees",
    )(*operands)


def local(
    columns_x,
    col_basis,
    col_links,
    col_top_links,
    row_basis,
    row_links,
    coupling,
    coupling_rows,
    coupling_cols,
    near_blocks,
    near_rows,
    near_cols,
):
    message = pl.pallas_call(
        moments_kernel,
        out_shape=jax.ShapeDtypeStruct((16, 48, 128), BF16),
        in_specs=[vmem()] * 3,
        out_specs=vmem(),
        name="moments",
    )(columns_x, col_basis, col_links)
    same_core = [[2 * chip + core for chip in CHIP_ORDER] for core in range(2)]
    same_chip = [[2 * chip, 2 * chip + 1] for chip in range(16)]
    arrived = lax.all_to_all(message, "row", 0, 0, axis_index_groups=same_core)
    blocks, up, down, rows, cols, nearby = call_prepare(
        coupling, col_top_links, row_links, coupling_rows, coupling_cols,
        near_blocks, columns_x, near_rows, near_cols,
    )
    arrived, nearby = lax.optimization_barrier((arrived, nearby))
    gathered = lax.all_gather(arrived, "row", axis=0, axis_index_groups=same_chip)
    partials = call_trees(rows, cols, gathered, up, blocks, down)
    same_row = [[16 * row + z for z in COL_ORDERS[row % 2]] for row in range(32)]
    scattered = lax.all_to_all(partials, ("row", "col"), 0, 0, axis_index_groups=same_row)
    return pl.pallas_call(
        output_kernel,
        out_shape=jax.ShapeDtypeStruct((32, 512), BF16),
        in_specs=[vmem()] * 3,
        out_specs=vmem(),
        compiler_params=pltpu.CompilerParams(vmem_limit_bytes=8 * 1024 * 1024),
        name="outputs",
    )(scattered, row_basis, nearby)


def solution(mesh):
    in_specs = (
        P(None, ("row", "col")),
        P(("row", "col"), None, None),
        P(("row", "col"), None),
        P("col", None, None),
        P(("row", "col"), None, None),
        P("row", None, None),
        P(("row", "col"), None),
        P(("row", "col"), None),
        P(("row", "col"), None),
        P(("row", "col"), None, None),
        P(("row", "col")),
        P(("row", "col")),
    )
    out_specs = P(None, ("row", "col"))
    return jax.shard_map(local, mesh=mesh, in_specs=in_specs, out_specs=out_specs, check_vma=False)
```

```python
import jax
import jax.numpy as jnp
from jax import lax
from jax.experimental import pallas as pl
from jax.experimental.pallas import tpu as pltpu
from jax.sharding import PartitionSpec as P

CHIP_ORDERS = [(10 + j) % 16 for j in range(16)], [(10 - j) % 16 for j in range(16)]
COL_ORDERS = [(11 + j) % 16 for j in range(16)], [(8 - j) % 16 for j in range(16)]

F32 = jnp.float32
BF16 = jnp.bfloat16


def dot(a, b):
    return jnp.dot(a, b, preferred_element_type=F32)


def vmem():
    return pl.BlockSpec(memory_space=pltpu.VMEM)


def smem():
    return pl.BlockSpec(memory_space=pltpu.SMEM)


def moments_kernel(x_ref, basis_ref, links_ref, out_ref):
    links = links_ref[...].reshape(2, 64, 64)
    leaves = []
    for i in range(2):
        moment = lax.dot_general(
            x_ref[:, 256 * i : 256 * (i + 1)],
            basis_ref[i],
            (((1,), (1,)), ((), ())),
            preferred_element_type=F32,
        )
        leaves.append(moment.astype(BF16))
    parent = dot(leaves[0], links[0]) + dot(leaves[1], links[1])
    low = jnp.concatenate(leaves, axis=1)
    high = jnp.concatenate([parent[:16], parent[16:]], axis=1).astype(BF16)
    for r in range(out_ref.shape[0]):
        out_ref[r, 0:32, :] = low
        out_ref[r, 32:48, :] = high


def paired(first, second):
    columns = []
    for i in range(0, first.shape[1], 128):
        one, two = first[:, i : i + 128], second[:, i : i + 128]
        columns.append(jnp.concatenate([one[:, 0:64], two[:, 0:64]], axis=1))
        columns.append(jnp.concatenate([one[:, 64:128], two[:, 64:128]], axis=1))
    return jnp.concatenate(columns, axis=1).reshape(first.shape[0], 64, 128)


def prepare_kernel(
    coupling_in, top_in, links_in, rows_in, cols_in, near_in, x_in, near_rows_in, near_cols_in,
    blocks_ref, up_ref, down_ref, rows_ref, cols_ref, nearby_ref,
    coupling_ref, top_ref, links_ref, near_ref, x_ref, near_rows_ref, near_cols_ref, sems,
):
    pairs = (
        (links_in.at[0], links_ref),
        (top_in.at[0], top_ref),
        (coupling_in, coupling_ref),
        (near_rows_in, near_rows_ref),
        (near_cols_in, near_cols_ref),
        (x_in, x_ref),
        (near_in, near_ref),
        (rows_in, rows_ref),
        (cols_in, cols_ref),
    )
    copies = [pltpu.make_async_copy(source, target, sems.at[i]) for i, (source, target) in enumerate(pairs)]
    for copy in copies:
        copy.start()
    copies[0].wait()
    links = links_ref[...].reshape(56, 64, 64)
    for b in range(16):
        one = jnp.concatenate([links[2 * b], links[2 * b + 1]], axis=1)
        two = dot(links[32 + b], one).astype(BF16)
        three = dot(links[48 + b // 2], two).astype(BF16)
        down_ref[b, 0:64, :] = two
        down_ref[b, 64:128, :] = one
        down_ref[b, 128:192, :] = jnp.zeros_like(one)
        down_ref[b, 192:256, :] = three
    copies[1].wait()
    top = top_ref[...].reshape(48, 64, 64)
    for p in range(24):
        up_ref[p] = jnp.concatenate([top[2 * p], top[2 * p + 1]], axis=1)
    copies[2].wait()
    for place, i in ((0, 0), (16, 16), (32, 64), (48, 80)):
        blocks_ref[place : place + 16] = paired(coupling_ref[i : i + 16], coupling_ref[i + 32 : i + 48])
    for copy in copies[3:7]:
        copy.wait()
    nearby_ref[...] = jnp.zeros_like(nearby_ref)
    for s in range(8):
        start = pl.multiple_of(near_cols_ref[s] * 256, 256)
        nearby_ref[near_rows_ref[s]] += dot(x_ref[:, pl.ds(start, 256)], near_ref[s])
    for copy in copies[7:]:
        copy.wait()


def tree_kernel(
    rows_ref, cols_ref, got_ref, top_ref, coupling_ref, down_ref, out_ref,
    mom0, mom1, mom2, mom3, acc0, acc1, acc2, acc3,
):
    mom, acc = (mom0, mom1, mom2, mom3), (acc0, acc1, acc2, acc3)
    for depth in range(4):
        acc[depth][...] = jnp.zeros_like(acc[depth])
    received = [(2 * CHIP_ORDERS[core][j] + core, core, j) for j in range(16) for core in range(2)]
    for a, core, j in received:
        parent = got_ref[core, j, 32:48, :]
        mom1[a, 0:16] = parent[:, 0:64]
        mom1[a, 16:32] = parent[:, 64:128]
    for p in range(16):
        both = dot(mom1[2 * p : 2 * p + 2].reshape(64, 64), top_ref[p])
        mom2[p] = (both[0:32, 0:64] + both[32:64, 64:128]).astype(BF16)
    for a, core, j in received:
        both = got_ref[core, j, 0:32, :]
        mom0[2 * a] = both[:, 0:64]
        mom0[2 * a + 1] = both[:, 64:128]
    for p in range(8):
        both = dot(mom2[2 * p : 2 * p + 2].reshape(64, 64), top_ref[16 + p])
        mom3[p] = (both[0:32, 0:64] + both[32:64, 64:128]).astype(BF16)
    for depth in (0, 2):
        for s in range(32):
            first, second = cols_ref[depth, s], cols_ref[depth + 1, s]
            picked = jnp.concatenate([mom[depth][first], mom[depth + 1][second]], axis=0)
            term = dot(picked, coupling_ref[depth * 16 + s])
            acc[depth][rows_ref[depth, s], :, 0:64] += term[0:32, 0:64]
            acc[depth + 1][rows_ref[depth + 1, s], :, 64:128] += term[32:64, 64:128]
    tops = [acc3[p].astype(BF16) for p in range(4)]
    core = lax.rem(lax.axis_index("row"), 2)
    for b in range(16):
        upper = jnp.concatenate([(acc1[b] + acc2[b // 2]).astype(BF16), tops[b // 4]], axis=1)
        own = jnp.concatenate([acc0[2 * b], acc0[2 * b + 1]], axis=1)
        place = jnp.where(core == 0, COL_ORDERS[0].index(b), COL_ORDERS[1].index(b))
        out_ref[place] = (own + dot(upper, down_ref[b])).astype(BF16)


def output_kernel(got_ref, basis_ref, near_ref, out_ref):
    total = got_ref[0].astype(F32)
    for b in range(1, got_ref.shape[0]):
        total += got_ref[b].astype(F32)
    leaf_local = total.astype(BF16)
    for i in range(2):
        distant = dot(leaf_local[:, 64 * i : 64 * (i + 1)], basis_ref[i])
        out_ref[:, 256 * i : 256 * (i + 1)] = (distant + near_ref[i]).astype(BF16)


def call_prepare(*operands):
    return pl.pallas_call(
        prepare_kernel,
        out_shape=[
            pltpu.VMEM((64, 64, 128), BF16),
            pltpu.VMEM((24, 64, 128), BF16),
            pltpu.VMEM((16, 256, 128), BF16),
            pltpu.SMEM((4, 32), jnp.int32),
            pltpu.SMEM((4, 32), jnp.int32),
            pltpu.VMEM((2, 32, 256), F32),
        ],
        in_specs=[pl.BlockSpec(memory_space=pl.ANY)] * 9,
        out_specs=[vmem()] * 3 + [smem()] * 2 + [vmem()],
        scratch_shapes=[
            pltpu.VMEM((128, 4096), BF16),
            pltpu.VMEM((48, 4096), BF16),
            pltpu.VMEM((56, 4096), BF16),
            pltpu.VMEM((8, 256, 256), BF16),
            pltpu.VMEM((32, 512), BF16),
            pltpu.SMEM((8,), jnp.int32),
            pltpu.SMEM((8,), jnp.int32),
            pltpu.SemaphoreType.DMA((9,)),
        ],
        compiler_params=pltpu.CompilerParams(vmem_limit_bytes=60 * 1024 * 1024),
        cost_estimate=pl.CostEstimate(flops=33_554_432, bytes_accessed=8_000_000, transcendentals=0),
        name="prepare",
    )(*operands)


def call_trees(*operands):
    return pl.pallas_call(
        tree_kernel,
        out_shape=jax.ShapeDtypeStruct((16, 32, 128), BF16),
        in_specs=[smem()] * 2 + [vmem()] * 4,
        out_specs=vmem(),
        scratch_shapes=[pltpu.VMEM((64 >> depth, 32, 64), BF16) for depth in range(4)]
        + [pltpu.VMEM((32 >> depth, 32, 128 if depth else 64), F32) for depth in range(4)],
        compiler_params=pltpu.CompilerParams(vmem_limit_bytes=16 * 1024 * 1024),
        name="trees",
    )(*operands)


def local(
    columns_x,
    col_basis,
    col_links,
    col_top_links,
    row_basis,
    row_links,
    coupling,
    coupling_rows,
    coupling_cols,
    near_blocks,
    near_rows,
    near_cols,
):
    message = pl.pallas_call(
        moments_kernel,
        out_shape=jax.ShapeDtypeStruct((16, 48, 128), BF16),
        in_specs=[vmem()] * 3,
        out_specs=vmem(),
        name="moments",
    )(columns_x, col_basis, col_links)
    same_core = [[2 * chip + core for chip in CHIP_ORDERS[core]] for core in range(2)]
    same_chip = [[2 * chip, 2 * chip + 1] for chip in range(16)]
    arrived = lax.all_to_all(message, "row", 0, 0, axis_index_groups=same_core)
    blocks, up, down, rows, cols, nearby = call_prepare(
        coupling, col_top_links, row_links, coupling_rows, coupling_cols,
        near_blocks, columns_x, near_rows, near_cols,
    )
    arrived, nearby = lax.optimization_barrier((arrived, nearby))
    gathered = lax.all_gather(arrived, "row", axis=0, axis_index_groups=same_chip)
    partials = call_trees(rows, cols, gathered, up, blocks, down)
    same_row = [[16 * row + z for z in COL_ORDERS[row % 2]] for row in range(32)]
    scattered = lax.all_to_all(partials, ("row", "col"), 0, 0, axis_index_groups=same_row)
    return pl.pallas_call(
        output_kernel,
        out_shape=jax.ShapeDtypeStruct((32, 512), BF16),
        in_specs=[vmem()] * 3,
        out_specs=vmem(),
        compiler_params=pltpu.CompilerParams(vmem_limit_bytes=8 * 1024 * 1024),
        name="outputs",
    )(scattered, row_basis, nearby)


def solution(mesh):
    in_specs = (
        P(None, ("row", "col")),
        P(("row", "col"), None, None),
        P(("row", "col"), None),
        P("col", None, None),
        P(("row", "col"), None, None),
        P("row", None, None),
        P(("row", "col"), None),
        P(("row", "col"), None),
        P(("row", "col"), None),
        P(("row", "col"), None, None),
        P(("row", "col")),
        P(("row", "col")),
    )
    out_specs = P(None, ("row", "col"))
    return jax.shard_map(local, mesh=mesh, in_specs=in_specs, out_specs=out_specs, check_vma=False)
```

```python
import jax
import jax.numpy as jnp
from jax import lax
from jax.experimental import pallas as pl
from jax.experimental.pallas import tpu as pltpu
from jax.sharding import PartitionSpec as P

CHIP_ORDER = [(10 + j) % 16 for j in range(16)]

F32 = jnp.float32
BF16 = jnp.bfloat16


def col_start(row):
    return 12 - 4 * (row % 2)


def dot(a, b):
    return jnp.dot(a, b, preferred_element_type=F32)


def vmem():
    return pl.BlockSpec(memory_space=pltpu.VMEM)


def smem():
    return pl.BlockSpec(memory_space=pltpu.SMEM)


def moments_kernel(x_ref, basis_ref, links_ref, out_ref):
    links = links_ref[...].reshape(2, 64, 64)
    leaves = []
    for i in range(2):
        moment = lax.dot_general(
            x_ref[:, 256 * i : 256 * (i + 1)],
            basis_ref[i],
            (((1,), (1,)), ((), ())),
            preferred_element_type=F32,
        )
        leaves.append(moment.astype(BF16))
    parent = dot(leaves[0], links[0]) + dot(leaves[1], links[1])
    low = jnp.concatenate(leaves, axis=1)
    high = jnp.concatenate([parent[:16], parent[16:]], axis=1).astype(BF16)
    for r in range(out_ref.shape[0]):
        out_ref[r, 0:32, :] = low
        out_ref[r, 32:48, :] = high


def paired(first, second):
    columns = []
    for i in range(0, first.shape[1], 128):
        one, two = first[:, i : i + 128], second[:, i : i + 128]
        columns.append(jnp.concatenate([one[:, 0:64], two[:, 0:64]], axis=1))
        columns.append(jnp.concatenate([one[:, 64:128], two[:, 64:128]], axis=1))
    return jnp.concatenate(columns, axis=1).reshape(first.shape[0], 64, 128)


def prepare_kernel(
    coupling_in, top_in, links_in, rows_in, cols_in, near_in, x_in, near_rows_in, near_cols_in,
    blocks_ref, up_ref, down_ref, rows_ref, cols_ref, nearby_ref,
    coupling_ref, top_ref, links_ref, near_ref, x_ref, near_rows_ref, near_cols_ref, sems,
):
    pairs = (
        (links_in.at[0], links_ref),
        (top_in.at[0], top_ref),
        (coupling_in, coupling_ref),
        (near_rows_in, near_rows_ref),
        (near_cols_in, near_cols_ref),
        (x_in, x_ref),
        (near_in, near_ref),
        (rows_in, rows_ref),
        (cols_in, cols_ref),
    )
    copies = [pltpu.make_async_copy(source, target, sems.at[i]) for i, (source, target) in enumerate(pairs)]
    for copy in copies:
        copy.start()
    copies[0].wait()
    links = links_ref[...].reshape(56, 64, 64)
    for b in range(16):
        one = jnp.concatenate([links[2 * b], links[2 * b + 1]], axis=1)
        two = dot(links[32 + b], one).astype(BF16)
        three = dot(links[48 + b // 2], two).astype(BF16)
        down_ref[b, 0:64, :] = two
        down_ref[b, 64:128, :] = one
        down_ref[b, 128:192, :] = jnp.zeros_like(one)
        down_ref[b, 192:256, :] = three
    copies[1].wait()
    top = top_ref[...].reshape(48, 64, 64)
    for p in range(24):
        up_ref[p] = jnp.concatenate([top[2 * p], top[2 * p + 1]], axis=1)
    copies[2].wait()
    for place, i in ((0, 0), (16, 16), (32, 64), (48, 80)):
        blocks_ref[place : place + 16] = paired(coupling_ref[i : i + 16], coupling_ref[i + 32 : i + 48])
    for copy in copies[3:7]:
        copy.wait()
    nearby_ref[...] = jnp.zeros_like(nearby_ref)
    for s in range(8):
        start = pl.multiple_of(near_cols_ref[s] * 256, 256)
        nearby_ref[near_rows_ref[s]] += dot(x_ref[:, pl.ds(start, 256)], near_ref[s])
    for copy in copies[7:]:
        copy.wait()


def tree_kernel(
    rows_ref, cols_ref, got_ref, top_ref, coupling_ref, down_ref, out_ref,
    mom0, mom1, mom2, mom3, acc0, acc1, acc2, acc3,
):
    mom, acc = (mom0, mom1, mom2, mom3), (acc0, acc1, acc2, acc3)
    for depth in range(4):
        acc[depth][...] = jnp.zeros_like(acc[depth])
    received = [(2 * chip + core, core, j) for j, chip in enumerate(CHIP_ORDER) for core in range(2)]
    for a, core, j in received:
        parent = got_ref[core, j, 32:48, :]
        mom1[a, 0:16] = parent[:, 0:64]
        mom1[a, 16:32] = parent[:, 64:128]
    for p in range(16):
        both = dot(mom1[2 * p : 2 * p + 2].reshape(64, 64), top_ref[p])
        mom2[p] = (both[0:32, 0:64] + both[32:64, 64:128]).astype(BF16)
    for a, core, j in received:
        both = got_ref[core, j, 0:32, :]
        mom0[2 * a] = both[:, 0:64]
        mom0[2 * a + 1] = both[:, 64:128]
    for p in range(8):
        both = dot(mom2[2 * p : 2 * p + 2].reshape(64, 64), top_ref[16 + p])
        mom3[p] = (both[0:32, 0:64] + both[32:64, 64:128]).astype(BF16)
    for depth in (0, 2):
        for s in range(32):
            first, second = cols_ref[depth, s], cols_ref[depth + 1, s]
            picked = jnp.concatenate([mom[depth][first], mom[depth + 1][second]], axis=0)
            term = dot(picked, coupling_ref[depth * 16 + s])
            acc[depth][rows_ref[depth, s], :, 0:64] += term[0:32, 0:64]
            acc[depth + 1][rows_ref[depth + 1, s], :, 64:128] += term[32:64, 64:128]
    tops = [acc3[p].astype(BF16) for p in range(4)]
    start = col_start(lax.axis_index("row"))
    for b in range(16):
        upper = jnp.concatenate([(acc1[b] + acc2[b // 2]).astype(BF16), tops[b // 4]], axis=1)
        own = jnp.concatenate([acc0[2 * b], acc0[2 * b + 1]], axis=1)
        out_ref[lax.rem(16 + b - start, 16)] = (own + dot(upper, down_ref[b])).astype(BF16)


def output_kernel(got_ref, basis_ref, near_ref, out_ref):
    total = got_ref[0].astype(F32)
    for b in range(1, got_ref.shape[0]):
        total += got_ref[b].astype(F32)
    leaf_local = total.astype(BF16)
    for i in range(2):
        distant = dot(leaf_local[:, 64 * i : 64 * (i + 1)], basis_ref[i])
        out_ref[:, 256 * i : 256 * (i + 1)] = (distant + near_ref[i]).astype(BF16)


def call_prepare(*operands):
    return pl.pallas_call(
        prepare_kernel,
        out_shape=[
            pltpu.VMEM((64, 64, 128), BF16),
            pltpu.VMEM((24, 64, 128), BF16),
            pltpu.VMEM((16, 256, 128), BF16),
            pltpu.SMEM((4, 32), jnp.int32),
            pltpu.SMEM((4, 32), jnp.int32),
            pltpu.VMEM((2, 32, 256), F32),
        ],
        in_specs=[pl.BlockSpec(memory_space=pl.ANY)] * 9,
        out_specs=[vmem()] * 3 + [smem()] * 2 + [vmem()],
        scratch_shapes=[
            pltpu.VMEM((128, 4096), BF16),
            pltpu.VMEM((48, 4096), BF16),
            pltpu.VMEM((56, 4096), BF16),
            pltpu.VMEM((8, 256, 256), BF16),
            pltpu.VMEM((32, 512), BF16),
            pltpu.SMEM((8,), jnp.int32),
            pltpu.SMEM((8,), jnp.int32),
            pltpu.SemaphoreType.DMA((9,)),
        ],
        compiler_params=pltpu.CompilerParams(vmem_limit_bytes=60 * 1024 * 1024),
        cost_estimate=pl.CostEstimate(flops=33_554_432, bytes_accessed=8_000_000, transcendentals=0),
        name="prepare",
    )(*operands)


def call_trees(*operands):
    return pl.pallas_call(
        tree_kernel,
        out_shape=jax.ShapeDtypeStruct((16, 32, 128), BF16),
        in_specs=[smem()] * 2 + [vmem()] * 4,
        out_specs=vmem(),
        scratch_shapes=[pltpu.VMEM((64 >> depth, 32, 64), BF16) for depth in range(4)]
        + [pltpu.VMEM((32 >> depth, 32, 128 if depth else 64), F32) for depth in range(4)],
        compiler_params=pltpu.CompilerParams(vmem_limit_bytes=16 * 1024 * 1024),
        name="trees",
    )(*operands)


def local(
    columns_x,
    col_basis,
    col_links,
    col_top_links,
    row_basis,
    row_links,
    coupling,
    coupling_rows,
    coupling_cols,
    near_blocks,
    near_rows,
    near_cols,
):
    message = pl.pallas_call(
        moments_kernel,
        out_shape=jax.ShapeDtypeStruct((16, 48, 128), BF16),
        in_specs=[vmem()] * 3,
        out_specs=vmem(),
        name="moments",
    )(columns_x, col_basis, col_links)
    same_core = [[2 * chip + core for chip in CHIP_ORDER] for core in range(2)]
    same_chip = [[2 * chip, 2 * chip + 1] for chip in range(16)]
    arrived = lax.all_to_all(message, "row", 0, 0, axis_index_groups=same_core)
    blocks, up, down, rows, cols, nearby = call_prepare(
        coupling, col_top_links, row_links, coupling_rows, coupling_cols,
        near_blocks, columns_x, near_rows, near_cols,
    )
    arrived, nearby = lax.optimization_barrier((arrived, nearby))
    gathered = lax.all_gather(arrived, "row", axis=0, axis_index_groups=same_chip)
    partials = call_trees(rows, cols, gathered, up, blocks, down)
    same_row = [[16 * row + (col_start(row) + j) % 16 for j in range(16)] for row in range(32)]
    scattered = lax.all_to_all(partials, ("row", "col"), 0, 0, axis_index_groups=same_row)
    return pl.pallas_call(
        output_kernel,
        out_shape=jax.ShapeDtypeStruct((32, 512), BF16),
        in_specs=[vmem()] * 3,
        out_specs=vmem(),
        compiler_params=pltpu.CompilerParams(vmem_limit_bytes=8 * 1024 * 1024),
        name="outputs",
    )(scattered, row_basis, nearby)


def solution(mesh):
    in_specs = (
        P(None, ("row", "col")),
        P(("row", "col"), None, None),
        P(("row", "col"), None),
        P("col", None, None),
        P(("row", "col"), None, None),
        P("row", None, None),
        P(("row", "col"), None),
        P(("row", "col"), None),
        P(("row", "col"), None),
        P(("row", "col"), None, None),
        P(("row", "col")),
        P(("row", "col")),
    )
    out_specs = P(None, ("row", "col"))
    return jax.shard_map(local, mesh=mesh, in_specs=in_specs, out_specs=out_specs, check_vma=False)
```

```python
import jax
import jax.numpy as jnp
from jax import lax
from jax.experimental import pallas as pl
from jax.experimental.pallas import tpu as pltpu
from jax.sharding import PartitionSpec as P

CHIP_ORDER = [(10 + j) % 16 for j in range(16)]

F32 = jnp.float32
BF16 = jnp.bfloat16


def col_start(row):
    return 12 - 4 * (row % 2) - (row < 1)


def dot(a, b):
    return jnp.dot(a, b, preferred_element_type=F32)


def vmem():
    return pl.BlockSpec(memory_space=pltpu.VMEM)


def smem():
    return pl.BlockSpec(memory_space=pltpu.SMEM)


def moments_kernel(x_ref, basis_ref, links_ref, out_ref):
    links = links_ref[...].reshape(2, 64, 64)
    leaves = []
    for i in range(2):
        moment = lax.dot_general(
            x_ref[:, 256 * i : 256 * (i + 1)],
            basis_ref[i],
            (((1,), (1,)), ((), ())),
            preferred_element_type=F32,
        )
        leaves.append(moment.astype(BF16))
    parent = dot(leaves[0], links[0]) + dot(leaves[1], links[1])
    low = jnp.concatenate(leaves, axis=1)
    high = jnp.concatenate([parent[:16], parent[16:]], axis=1).astype(BF16)
    for r in range(out_ref.shape[0]):
        out_ref[r, 0:32, :] = low
        out_ref[r, 32:48, :] = high


def paired(first, second):
    columns = []
    for i in range(0, first.shape[1], 128):
        one, two = first[:, i : i + 128], second[:, i : i + 128]
        columns.append(jnp.concatenate([one[:, 0:64], two[:, 0:64]], axis=1))
        columns.append(jnp.concatenate([one[:, 64:128], two[:, 64:128]], axis=1))
    return jnp.concatenate(columns, axis=1).reshape(first.shape[0], 64, 128)


def prepare_kernel(
    coupling_in, top_in, links_in, rows_in, cols_in, near_in, x_in, near_rows_in, near_cols_in,
    blocks_ref, up_ref, down_ref, rows_ref, cols_ref, nearby_ref,
    coupling_ref, top_ref, links_ref, near_ref, x_ref, near_rows_ref, near_cols_ref, sems,
):
    pairs = (
        (links_in.at[0], links_ref),
        (top_in.at[0], top_ref),
        (coupling_in, coupling_ref),
        (near_rows_in, near_rows_ref),
        (near_cols_in, near_cols_ref),
        (x_in, x_ref),
        (near_in, near_ref),
        (rows_in, rows_ref),
        (cols_in, cols_ref),
    )
    copies = [pltpu.make_async_copy(source, target, sems.at[i]) for i, (source, target) in enumerate(pairs)]
    for copy in copies:
        copy.start()
    copies[0].wait()
    links = links_ref[...].reshape(56, 64, 64)
    for b in range(16):
        one = jnp.concatenate([links[2 * b], links[2 * b + 1]], axis=1)
        two = dot(links[32 + b], one).astype(BF16)
        three = dot(links[48 + b // 2], two).astype(BF16)
        down_ref[b, 0:64, :] = two
        down_ref[b, 64:128, :] = one
        down_ref[b, 128:192, :] = jnp.zeros_like(one)
        down_ref[b, 192:256, :] = three
    copies[1].wait()
    top = top_ref[...].reshape(48, 64, 64)
    for p in range(24):
        up_ref[p] = jnp.concatenate([top[2 * p], top[2 * p + 1]], axis=1)
    copies[2].wait()
    for place, i in ((0, 0), (16, 16), (32, 64), (48, 80)):
        blocks_ref[place : place + 16] = paired(coupling_ref[i : i + 16], coupling_ref[i + 32 : i + 48])
    for copy in copies[3:7]:
        copy.wait()
    nearby_ref[...] = jnp.zeros_like(nearby_ref)
    for s in range(8):
        start = pl.multiple_of(near_cols_ref[s] * 256, 256)
        nearby_ref[near_rows_ref[s]] += dot(x_ref[:, pl.ds(start, 256)], near_ref[s])
    for copy in copies[7:]:
        copy.wait()


def tree_kernel(
    rows_ref, cols_ref, got_ref, top_ref, coupling_ref, down_ref, out_ref,
    mom0, mom1, mom2, mom3, acc0, acc1, acc2, acc3,
):
    mom, acc = (mom0, mom1, mom2, mom3), (acc0, acc1, acc2, acc3)
    for depth in range(4):
        acc[depth][...] = jnp.zeros_like(acc[depth])
    received = [(2 * chip + core, core, j) for j, chip in enumerate(CHIP_ORDER) for core in range(2)]
    for a, core, j in received:
        parent = got_ref[core, j, 32:48, :]
        mom1[a, 0:16] = parent[:, 0:64]
        mom1[a, 16:32] = parent[:, 64:128]
    for p in range(16):
        both = dot(mom1[2 * p : 2 * p + 2].reshape(64, 64), top_ref[p])
        mom2[p] = (both[0:32, 0:64] + both[32:64, 64:128]).astype(BF16)
    for a, core, j in received:
        both = got_ref[core, j, 0:32, :]
        mom0[2 * a] = both[:, 0:64]
        mom0[2 * a + 1] = both[:, 64:128]
    for p in range(8):
        both = dot(mom2[2 * p : 2 * p + 2].reshape(64, 64), top_ref[16 + p])
        mom3[p] = (both[0:32, 0:64] + both[32:64, 64:128]).astype(BF16)
    for depth in (0, 2):
        for s in range(32):
            first, second = cols_ref[depth, s], cols_ref[depth + 1, s]
            picked = jnp.concatenate([mom[depth][first], mom[depth + 1][second]], axis=0)
            term = dot(picked, coupling_ref[depth * 16 + s])
            acc[depth][rows_ref[depth, s], :, 0:64] += term[0:32, 0:64]
            acc[depth + 1][rows_ref[depth + 1, s], :, 64:128] += term[32:64, 64:128]
    tops = [acc3[p].astype(BF16) for p in range(4)]
    start = col_start(lax.axis_index("row"))
    for b in range(16):
        upper = jnp.concatenate([(acc1[b] + acc2[b // 2]).astype(BF16), tops[b // 4]], axis=1)
        own = jnp.concatenate([acc0[2 * b], acc0[2 * b + 1]], axis=1)
        out_ref[lax.rem(16 + b - start, 16)] = (own + dot(upper, down_ref[b])).astype(BF16)


def output_kernel(got_ref, basis_ref, near_ref, out_ref):
    total = got_ref[0].astype(F32)
    for b in range(1, got_ref.shape[0]):
        total += got_ref[b].astype(F32)
    leaf_local = total.astype(BF16)
    for i in range(2):
        distant = dot(leaf_local[:, 64 * i : 64 * (i + 1)], basis_ref[i])
        out_ref[:, 256 * i : 256 * (i + 1)] = (distant + near_ref[i]).astype(BF16)


def call_prepare(*operands):
    return pl.pallas_call(
        prepare_kernel,
        out_shape=[
            pltpu.VMEM((64, 64, 128), BF16),
            pltpu.VMEM((24, 64, 128), BF16),
            pltpu.VMEM((16, 256, 128), BF16),
            pltpu.SMEM((4, 32), jnp.int32),
            pltpu.SMEM((4, 32), jnp.int32),
            pltpu.VMEM((2, 32, 256), F32),
        ],
        in_specs=[pl.BlockSpec(memory_space=pl.ANY)] * 9,
        out_specs=[vmem()] * 3 + [smem()] * 2 + [vmem()],
        scratch_shapes=[
            pltpu.VMEM((128, 4096), BF16),
            pltpu.VMEM((48, 4096), BF16),
            pltpu.VMEM((56, 4096), BF16),
            pltpu.VMEM((8, 256, 256), BF16),
            pltpu.VMEM((32, 512), BF16),
            pltpu.SMEM((8,), jnp.int32),
            pltpu.SMEM((8,), jnp.int32),
            pltpu.SemaphoreType.DMA((9,)),
        ],
        compiler_params=pltpu.CompilerParams(vmem_limit_bytes=60 * 1024 * 1024),
        cost_estimate=pl.CostEstimate(flops=33_554_432, bytes_accessed=8_000_000, transcendentals=0),
        name="prepare",
    )(*operands)


def call_trees(*operands):
    return pl.pallas_call(
        tree_kernel,
        out_shape=jax.ShapeDtypeStruct((16, 32, 128), BF16),
        in_specs=[smem()] * 2 + [vmem()] * 4,
        out_specs=vmem(),
        scratch_shapes=[pltpu.VMEM((64 >> depth, 32, 64), BF16) for depth in range(4)]
        + [pltpu.VMEM((32 >> depth, 32, 128 if depth else 64), F32) for depth in range(4)],
        compiler_params=pltpu.CompilerParams(vmem_limit_bytes=16 * 1024 * 1024),
        name="trees",
    )(*operands)


def local(
    columns_x,
    col_basis,
    col_links,
    col_top_links,
    row_basis,
    row_links,
    coupling,
    coupling_rows,
    coupling_cols,
    near_blocks,
    near_rows,
    near_cols,
):
    message = pl.pallas_call(
        moments_kernel,
        out_shape=jax.ShapeDtypeStruct((16, 48, 128), BF16),
        in_specs=[vmem()] * 3,
        out_specs=vmem(),
        name="moments",
    )(columns_x, col_basis, col_links)
    same_core = [[2 * chip + core for chip in CHIP_ORDER] for core in range(2)]
    same_chip = [[2 * chip, 2 * chip + 1] for chip in range(16)]
    arrived = lax.all_to_all(message, "row", 0, 0, axis_index_groups=same_core)
    blocks, up, down, rows, cols, nearby = call_prepare(
        coupling, col_top_links, row_links, coupling_rows, coupling_cols,
        near_blocks, columns_x, near_rows, near_cols,
    )
    arrived, nearby = lax.optimization_barrier((arrived, nearby))
    gathered = lax.all_gather(arrived, "row", axis=0, axis_index_groups=same_chip)
    partials = call_trees(rows, cols, gathered, up, blocks, down)
    same_row = [[16 * row + (col_start(row) + j) % 16 for j in range(16)] for row in range(32)]
    scattered = lax.all_to_all(partials, ("row", "col"), 0, 0, axis_index_groups=same_row)
    return pl.pallas_call(
        output_kernel,
        out_shape=jax.ShapeDtypeStruct((32, 512), BF16),
        in_specs=[vmem()] * 3,
        out_specs=vmem(),
        compiler_params=pltpu.CompilerParams(vmem_limit_bytes=8 * 1024 * 1024),
        name="outputs",
    )(scattered, row_basis, nearby)


def solution(mesh):
    in_specs = (
        P(None, ("row", "col")),
        P(("row", "col"), None, None),
        P(("row", "col"), None),
        P("col", None, None),
        P(("row", "col"), None, None),
        P("row", None, None),
        P(("row", "col"), None),
        P(("row", "col"), None),
        P(("row", "col"), None),
        P(("row", "col"), None, None),
        P(("row", "col")),
        P(("row", "col")),
    )
    out_specs = P(None, ("row", "col"))
    return jax.shard_map(local, mesh=mesh, in_specs=in_specs, out_specs=out_specs, check_vma=False)
```
